512 devices in a mesh: dp: 32 (over z, core), tensor: 16 (over x, y).
Axes of the slice: x: 4, y: 4, z: 16, core: 2. Of those that a mesh axis runs over, the one named last changes fastest.
Arguments:
- queries: bfloat16 [128, 16, 16384], P('dp', None, 'tensor'), may hold values from -18 to 18
- tree_kv: bfloat16 [128, 16, 8, 256], P('dp'), may hold values from -20 to 20
- prefix_kv: bfloat16 [32, 16, 1024, 256], P('dp', 'tensor'), may hold values from -20 to 20
- request_holder: int32 [128], replicated, may hold values from 0 to 31, as said below
- parents: int32 [128, 16], replicated, may hold values from 0 to 14, as said below
- out_weight: bfloat16 [16384, 16384], P('tensor', 'dp'), may hold values from -0.5 to 0.5
Outputs:
- projected: bfloat16 [128, 16, 16384], P('tensor', None, 'dp')
The draws below stay inside these ranges and needn't reach their ends.
Inputs may be any that keep to these rules, and one draw needn't show every extreme that they name: `request_holder`: each group serves at most 16 requests, and one group serves exactly 16. parents[r, 0] = 0 and parents[r, i] < i for i >= 1.
All inputs are finite; a program needn't handle non-finite values.
Results may differ from the reference program's by a relative error of at most 0.01785.
Values may be sent and summed in bfloat16 or wider, within the bound.
No kernel may reach another device: no remote copies, remote signals or barrier semaphores. Data moves between devices by JAX's collectives and lax.ppermute only.
A program may use at most 64 MiB of HBM per device.

```python
import math
import jax
import jax.numpy as jnp
from jax import lax

D = 16384
HD = 128
HEADS = 128
KVH = 8
NODES = 16
HALF = 1024
REQUESTS = 128
CAP = 16
N_DP = 32
N_TENSOR = 16


def shared_direction(key):
    return jnp.clip(jax.random.normal(jax.random.fold_in(key, 7), (HD,), jnp.float32), -2.5, 2.5)


def draw_queries(key, part):
    direction = shared_direction(key)
    key = jax.random.fold_in(key, 1)
    base_key = jax.random.fold_in(key, 0)
    shape = (REQUESTS, NODES, HEADS, HD)
    noise = 1.5 * jnp.clip(jax.random.normal(base_key, shape, jnp.float32), -4.0, 4.0)
    boost = jnp.zeros((REQUESTS,), jnp.float32)
    total = noise + (0.45 + boost)[:, None, None, None] * direction
    return total.reshape(REQUESTS, NODES, HEADS * HD).astype(jnp.bfloat16)


def draw_tree_kv(key, part):
    direction = shared_direction(key)
    key = jax.random.fold_in(key, 2)
    shape = (REQUESTS, NODES, KVH, 2 * HD)
    noise = jnp.clip(jax.random.normal(key, shape, jnp.float32), -4.0, 4.0)
    lift = jnp.concatenate([0.45 * direction, jnp.zeros((HD,), jnp.float32)])
    return (noise + lift).astype(jnp.bfloat16)


def draw_prefix_kv(key, part):
    key = jax.random.fold_in(key, 4)
    base_key = jax.random.fold_in(key, 0)
    shape = (N_DP, N_TENSOR, HALF, 2 * HD)
    noise = jnp.clip(jax.random.normal(base_key, shape, jnp.float32), -4.0, 4.0)
    return noise.astype(jnp.bfloat16)


def draw_request_holder(key, part):
    key = jax.random.fold_in(key, 3)
    first, second, third, fourth = jax.random.split(key, 4)
    busiest = jax.random.randint(first, (), 0, N_DP)
    others = N_DP - 1
    popular = jax.random.randint(second, (others,), 0, 4)
    seat_group = jnp.repeat(jnp.arange(others, dtype=jnp.int32), CAP)
    seat = jnp.tile(jnp.arange(CAP, dtype=jnp.int32), others)
    noise = jax.random.randint(third, (others * CAP,), 0, 1024)
    score = (popular[seat_group] * 1024 + noise - seat * 256) * (others * CAP) + jnp.arange(others * CAP, dtype=jnp.int32)
    chosen = lax.top_k(score, REQUESTS - CAP)[1]
    chosen_groups = (busiest + 1 + seat_group[chosen]) % N_DP
    assigned = jnp.concatenate([jnp.full((CAP,), busiest, jnp.int32), chosen_groups.astype(jnp.int32)])
    order = jax.random.permutation(fourth, REQUESTS)
    return assigned[order]


def draw_parents(key, part):
    key = jax.random.fold_in(key, 5)
    upper = jnp.maximum(jnp.arange(NODES, dtype=jnp.int32), 1)
    drawn = jax.random.randint(key, (REQUESTS, NODES), 0, upper[None, :]).astype(jnp.int32)
    return drawn.at[0, NODES - 1].set(NODES - 2)


def block_scale(rng, dims, shards, low, high):
    gain = 1.0
    for axis_at, shards_of in shards:
        draws = jax.random.uniform(jax.random.fold_in(jax.random.fold_in(rng, 6), axis_at), (shards_of,), jnp.float32, low / len(shards), high / len(shards))
        gain = gain * jnp.repeat(jnp.exp(draws), dims[axis_at] // shards_of).reshape((-1,) + (1,) * (len(dims) - 1 - axis_at))
    return gain


def normal_values(rng, dims, scale, bound, cuts=(), held_as=jnp.bfloat16):
    gain = block_scale(rng, dims, cuts, -0.22, 0.18) if cuts else 1.0
    values = jax.random.normal(rng, dims, jnp.float32) * scale * gain
    return jnp.minimum(jnp.maximum(values, -bound), bound).astype(held_as)


def setup_inputs(seed: int = 0) -> dict:
    arg_keys = jax.random.split(jax.random.key(seed), 7)
    return {
        "queries": draw_queries(jax.random.fold_in(arg_keys[6], 71), 0),
        "tree_kv": draw_tree_kv(jax.random.fold_in(arg_keys[6], 71), 0),
        "prefix_kv": draw_prefix_kv(jax.random.fold_in(arg_keys[6], 71), 0),
        "request_holder": draw_request_holder(jax.random.fold_in(arg_keys[6], 71), 0),
        "parents": draw_parents(jax.random.fold_in(arg_keys[6], 71), 0),
        "out_weight": normal_values(arg_keys[5], (HEADS * HD, D), HD ** -0.5, 0.5, ((0, 16), (1, 32))),
    }


def ancestors(parents):
    count = parents.shape[-1]
    ident = jnp.eye(count, dtype=jnp.int32)
    upward = (parents[..., None] == jnp.arange(count, dtype=jnp.int32)[None, None, :]).astype(jnp.int32)
    reach = jnp.minimum(ident[None] + upward, 1)
    for level in range(4):
        reach = jnp.minimum(jnp.einsum('rij,rjk->rik', reach, reach), 1)
    return reach

def attend_one(inputs, prefix_kv):
    query, tree_one, reach_one, holder = inputs
    kv_heads = tree_one.shape[1]
    group_size = HEADS // kv_heads
    whole = lax.dynamic_index_in_dim(prefix_kv, holder, 0, keepdims=False)
    whole = whole.reshape(kv_heads, 2 * HALF, 2 * HD).astype(jnp.float32)
    qf = query.astype(jnp.float32).reshape(NODES, kv_heads, group_size, HD)
    scale = 1.0 / math.sqrt(HD)
    pre_scores = jnp.einsum('nchd,cpd->nchp', qf, whole[..., :HD]) * scale
    tree_f = tree_one.astype(jnp.float32)
    tree_scores = jnp.einsum('nchd,jcd->nchj', qf, tree_f[..., :HD]) * scale
    mask = (reach_one > 0)[:, None, None, :]
    tree_scores = jnp.where(mask, tree_scores, jnp.float32(-1e+30))
    top = jnp.maximum(lax.optimization_barrier(jnp.max(pre_scores, axis=-1)), lax.optimization_barrier(jnp.max(tree_scores, axis=-1)))
    pre_w = jnp.exp(pre_scores - top[..., None])
    tree_w = jnp.exp(tree_scores - top[..., None]) * mask.astype(jnp.float32)
    total = lax.optimization_barrier(jnp.sum(pre_w, axis=-1)) + lax.optimization_barrier(jnp.sum(tree_w, axis=-1))
    pre_b = pre_w.astype(jnp.bfloat16).astype(jnp.float32)
    tree_b = tree_w.astype(jnp.bfloat16).astype(jnp.float32)
    summed = jnp.einsum('nchp,cpd->nchd', pre_b, whole[..., HD:]) + jnp.einsum('nchj,jcd->nchd', tree_b, tree_f[..., HD:])
    out = summed / total[..., None]
    return out.reshape(NODES, HEADS * HD).astype(jnp.bfloat16)

def reference(queries, tree_kv, prefix_kv, request_holder, parents, out_weight):
    reach = ancestors(parents)
    attended = lax.map(lambda item: attend_one(item, prefix_kv), (queries, tree_kv, reach, request_holder))
    flat = attended.reshape(REQUESTS * NODES, HEADS * HD)
    result = jnp.dot(flat, out_weight, preferred_element_type=jnp.float32)
    return result.reshape(REQUESTS, NODES, D).astype(jnp.bfloat16)
```

```python
import math

import jax
import jax.numpy as jnp
from jax import lax
from jax.experimental import pallas as pl
from jax.experimental.pallas import tpu as pltpu
from jax.sharding import PartitionSpec as P

CAP = 16
PAIR = 2
NEG = -1e30


def swapped(x, axis, bit):
    return lax.ppermute(x, axis, [(i, i ^ 1 << bit) for i in range(lax.axis_size(axis))])


def attend_kernel(index_ref, parent_ref, first_ref, second_ref, own_ref, other_ref, out_ref, reach_ref, value_ref):
    step = pl.program_id(0)
    nodes = first_ref.shape[1]
    width = own_ref.shape[1] // 2
    heads = (first_ref.shape[2] - 2 * width) // width
    half = own_ref.shape[0]
    rows = CAP * nodes

    @pl.when(step == 0)
    def _():
        line = lax.broadcasted_iota(jnp.int32, (rows, rows), 0)
        column = lax.broadcasted_iota(jnp.int32, (rows, rows), 1)
        above = (line // nodes) * nodes + parent_ref[...]
        reach = jnp.where((column == line) | (column == above), 1.0, 0.0).astype(jnp.bfloat16)
        for level in range(4):
            reach = jnp.minimum(
                jnp.dot(reach, reach, preferred_element_type=jnp.float32), 1.0
            ).astype(jnp.bfloat16)
        reach_ref[...] = reach.astype(jnp.float32)
        value_ref[pl.ds(0, half), :width] = own_ref[:, width:]
        value_ref[pl.ds(half, half), :width] = other_ref[:, width:]
        value_ref[:, width:] = jnp.ones((2 * half, width), jnp.bfloat16)

    scale = 1.0 / math.sqrt(width) * math.log2(math.e)
    refs = (first_ref, second_ref)
    query = jnp.concatenate(
        [ref[0, :, h * width : (h + 1) * width] for ref in refs for h in range(heads)], axis=0
    )
    tree = jnp.concatenate([ref[0, :, heads * width :] for ref in refs], axis=0)
    dims = (((1,), (1,)), ((), ()))
    near = lax.dot_general(query, own_ref[:, :width], dims, preferred_element_type=jnp.float32)
    far = lax.dot_general(query, other_ref[:, :width], dims, preferred_element_type=jnp.float32)
    drafts = lax.dot_general(query, tree[:, :width], dims, preferred_element_type=jnp.float32)
    span = PAIR * nodes
    mask = jnp.zeros((span, span), jnp.float32)
    for k in range(CAP // PAIR):
        block = reach_ref[k * span : (k + 1) * span, k * span : (k + 1) * span]
        mask = jnp.where(step == k, block, mask)
    mask = jnp.concatenate(
        [mask[s * nodes : (s + 1) * nodes] for s in range(PAIR) for h in range(heads)], axis=0
    )
    drafts = jnp.where(mask > 0, drafts, NEG)
    top = jnp.maximum(
        jnp.maximum(jnp.max(near, axis=1, keepdims=True), jnp.max(far, axis=1, keepdims=True)),
        jnp.max(drafts, axis=1, keepdims=True),
    )
    near = jnp.exp2((near - top) * scale).astype(jnp.bfloat16)
    far = jnp.exp2((far - top) * scale).astype(jnp.bfloat16)
    drafts = (jnp.exp2((drafts - top) * scale) * mask).astype(jnp.bfloat16)
    tree_value = jnp.concatenate([tree[:, width:], jnp.ones((span, width), jnp.bfloat16)], axis=1)
    summed = (
        jnp.dot(near, value_ref[pl.ds(0, half), :], preferred_element_type=jnp.float32)
        + jnp.dot(far, value_ref[pl.ds(half, half), :], preferred_element_type=jnp.float32)
        + jnp.dot(drafts, tree_value, preferred_element_type=jnp.float32)
    )
    attended = (summed[:, :width] / summed[:, width:]).astype(jnp.bfloat16)
    for s in range(PAIR):
        for h in range(heads):
            start = (s * heads + h) * nodes
            out_ref[s, :, h * width : (h + 1) * width] = attended[start : start + nodes]


def attend(index, parent, packed, own, other):
    nodes = packed.shape[1]
    depth = packed.shape[2]
    width = own.shape[1] // 2
    half = own.shape[0]
    model = depth - 2 * width
    return pl.pallas_call(
        attend_kernel,
        out_shape=jax.ShapeDtypeStruct((CAP, nodes, model), jnp.bfloat16),
        grid_spec=pltpu.PrefetchScalarGridSpec(
            num_scalar_prefetch=1,
            grid=(CAP // PAIR,),
            in_specs=[
                pl.BlockSpec((CAP * nodes, 1), lambda i, index: (0, 0)),
                pl.BlockSpec((1, nodes, depth), lambda i, index: (index[PAIR * i], 0, 0)),
                pl.BlockSpec((1, nodes, depth), lambda i, index: (index[PAIR * i + 1], 0, 0)),
                pl.BlockSpec((half, 2 * width), lambda i, index: (0, 0)),
                pl.BlockSpec((half, 2 * width), lambda i, index: (0, 0)),
            ],
            out_specs=pl.BlockSpec((PAIR, nodes, model), lambda i, index: (i, 0, 0)),
            scratch_shapes=[
                pltpu.VMEM((CAP * nodes, CAP * nodes), jnp.float32),
                pltpu.VMEM((2 * half, 2 * width), jnp.bfloat16),
            ],
        ),
        compiler_params=pltpu.CompilerParams(vmem_limit_bytes=40 * 1024 * 1024),
        name="attend",
    )(index, parent, packed, packed, own, other)


def project_kernel(place_ref, every_ref, weight_ref, out_ref, rows_ref, sems):
    lanes, depth = out_ref.shape[0], weight_ref.shape[0]
    requests, nodes = rows_ref.shape[0], rows_ref.shape[1]
    share = requests // lanes
    copies = []
    for r in range(requests):
        copy = pltpu.make_async_copy(every_ref.at[place_ref[r]], rows_ref.at[r], sems.at[r])
        copy.start()
        copies.append(copy)
    for lane in range(lanes):
        for copy in copies[lane * share : (lane + 1) * share]:
            copy.wait()
        block = rows_ref[lane * share : (lane + 1) * share].reshape(share * nodes, depth)
        out_ref[lane] = jnp.dot(
            block, weight_ref[...], preferred_element_type=jnp.float32
        ).astype(jnp.bfloat16)


def project(place, every, weight, lanes):
    requests = place.shape[0]
    nodes, depth = every.shape[1], every.shape[2]
    columns = weight.shape[1]
    return pl.pallas_call(
        project_kernel,
        out_shape=jax.ShapeDtypeStruct((lanes, requests // lanes * nodes, columns), jnp.bfloat16),
        grid_spec=pltpu.PrefetchScalarGridSpec(
            num_scalar_prefetch=1,
            grid=(),
            in_specs=[
                pl.BlockSpec(memory_space=pl.ANY),
                pl.BlockSpec(memory_space=pltpu.VMEM),
            ],
            out_specs=pl.BlockSpec(memory_space=pltpu.VMEM),
            scratch_shapes=[
                pltpu.VMEM((requests, nodes, depth), jnp.bfloat16),
                pltpu.SemaphoreType.DMA((requests,)),
            ],
        ),
        compiler_params=pltpu.CompilerParams(vmem_limit_bytes=40 * 1024 * 1024),
        name="project",
    )(place, every, weight)


def local(queries, tree_kv, prefix_kv, request_holder, parents, out_weight):
    group = lax.axis_index("dp")
    lane = lax.axis_index("tensor")
    lanes = lax.axis_size("tensor")
    requests = request_holder.shape[0]
    nodes = queries.shape[1]
    tree_local = lax.dynamic_index_in_dim(tree_kv, lane // 2, 2, keepdims=False)
    packed = lax.all_gather(
        jnp.concatenate([queries, tree_local], axis=2), "dp", axis=0, tiled=True
    )
    own_half = prefix_kv[0, 0]
    other_half = swapped(own_half, "tensor", 0)
    order = jnp.arange(requests, dtype=jnp.int32)
    same = request_holder[:, None] == request_holder[None, :]
    rank = jnp.sum((same & (order[None, :] < order[:, None])).astype(jnp.int32), axis=1)
    slots = jnp.arange(CAP, dtype=jnp.int32)
    pick = ((request_holder[None, :] == group) & (rank[None, :] == slots[:, None])).astype(jnp.int32)
    index = jnp.sum(pick * order[None, :], axis=1)
    slot_parents = jnp.sum(pick[:, :, None] * parents[None], axis=1).reshape(CAP * nodes, 1)
    attended = attend(index, slot_parents, packed, own_half, other_half)
    every = lax.all_gather(attended, "dp", axis=0, tiled=True)
    partial = project(request_holder * CAP + rank, every, out_weight, lanes)
    shares = lax.all_to_all(partial, "tensor", 0, 0, tiled=True)
    total = jnp.sum(shares.astype(jnp.float32), axis=0).astype(jnp.bfloat16)
    return total.reshape(requests // lanes, nodes, out_weight.shape[1])


def solution(mesh):
    return jax.shard_map(
        local,
        mesh=mesh,
        in_specs=(
            P("dp", None, "tensor"),
            P("dp", None, None, None),
            P("dp", "tensor", None, None),
            P(),
            P(),
            P("tensor", "dp"),
        ),
        out_specs=P("tensor", None, "dp"),
        check_vma=False,
    )
```

```python
import math

import jax
import jax.numpy as jnp
from jax import lax
from jax.experimental import pallas as pl
from jax.experimental.pallas import tpu as pltpu
from jax.sharding import PartitionSpec as P

CAP = 16
PAIR = 2
NEG = -1e30
RAISE = 2.0**11


def swapped(x, axis, bit):
    return lax.ppermute(x, axis, [(i, i ^ 1 << bit) for i in range(lax.axis_size(axis))])


def exponent(x):
    peak = jnp.max(jnp.abs(x), axis=-1, keepdims=True)
    return jnp.floor(jnp.log2(jnp.clip(peak, 2.0**-100, 2.0**6)))


def pack_kernel(place_ref, queries_ref, tree_ref, holder_ref, packed_ref, slot_ref, index_ref, place_out_ref):
    group, column = place_ref[0], place_ref[1]
    count, nodes, model = queries_ref.shape
    kv_heads, width = tree_ref.shape[2], tree_ref.shape[3] // 2
    pick = lax.broadcasted_iota(jnp.int32, (nodes, kv_heads, 2 * width), 1) == column
    for r in range(count):
        packed_ref[r, :, :model] = (queries_ref[r].astype(jnp.float32) * RAISE).astype(jnp.bfloat16)
        tree = jnp.sum(jnp.where(pick, tree_ref[r].astype(jnp.float32), 0.0), axis=1)
        packed_ref[r, :, model : model + width] = (tree[:, :width] * RAISE).astype(jnp.bfloat16)
        values = tree[:, width:]
        power = exponent(values)
        packed_ref[r, :, model + width : model + 2 * width] = (
            values * jnp.exp2(10.0 - power)
        ).astype(jnp.bfloat16)
        packed_ref[r, :, model + 2 * width :] = jnp.broadcast_to(power, values.shape).astype(
            jnp.bfloat16
        )
    requests = holder_ref.shape[1]
    line = lax.broadcasted_iota(jnp.int32, (requests, requests), 0)
    lane = lax.broadcasted_iota(jnp.int32, (requests, requests), 1)
    row = holder_ref[...]
    rows = jnp.broadcast_to(row, (requests, requests))
    column = jnp.sum(jnp.where(line == lane, rows, 0), axis=1, keepdims=True)
    before = jnp.where((column == rows) & (line < lane), 1, 0)
    rank = jnp.sum(before, axis=0, keepdims=True)
    after = jnp.where((column == rows) & (lane < line), 1, 0)
    rank_column = jnp.sum(after, axis=1, keepdims=True)
    slot_ref[...] = jnp.where(row == group, rank, -1)
    place_out_ref[...] = row * CAP + rank
    mine = (column == group) & (rank_column == lane)
    index_ref[...] = jnp.sum(jnp.where(mine, line, 0), axis=0, keepdims=True)


def pack(place, queries, tree, holder):
    count, nodes, model = queries.shape
    width = tree.shape[3] // 2
    requests = holder.shape[0]
    vmem = pl.BlockSpec(memory_space=pltpu.VMEM)
    line = jax.ShapeDtypeStruct((1, requests), jnp.int32)
    return pl.pallas_call(
        pack_kernel,
        out_shape=(
            jax.ShapeDtypeStruct((count, nodes, model + 3 * width), jnp.bfloat16),
            line,
            line,
            line,
        ),
        grid_spec=pltpu.PrefetchScalarGridSpec(
            num_scalar_prefetch=1, grid=(), in_specs=[vmem] * 3, out_specs=(vmem,) * 4
        ),
        compiler_params=pltpu.CompilerParams(vmem_limit_bytes=40 * 1024 * 1024),
        name="pack",
    )(place, queries, tree, holder.reshape(1, requests))


def attend_kernel(slot_ref, parents_ref, picked_ref, own_ref, other_ref, out_ref, reach_ref, value_ref):
    step = pl.program_id(0)
    nodes = picked_ref.shape[1]
    width = own_ref.shape[1] // 2
    heads = (picked_ref.shape[2] - 3 * width) // width
    half = own_ref.shape[0]
    rows = CAP * nodes

    @pl.when(step == 0)
    def _():
        line = lax.broadcasted_iota(jnp.int32, (rows, rows), 0)
        column = lax.broadcasted_iota(jnp.int32, (rows, rows), 1)
        requests = slot_ref.shape[1]
        taken = lax.broadcasted_iota(jnp.int32, (rows, requests), 0) // nodes == slot_ref[...]
        above = jnp.dot(
            jnp.where(taken, 1.0, 0.0).astype(jnp.bfloat16),
            parents_ref[...].astype(jnp.float32).astype(jnp.bfloat16),
            preferred_element_type=jnp.float32,
        )
        node = lax.broadcasted_iota(jnp.int32, (rows, nodes), 0) % nodes
        own_node = lax.broadcasted_iota(jnp.int32, (rows, nodes), 1) == node
        above = jnp.sum(jnp.where(own_node, above, 0.0), axis=1, keepdims=True).astype(jnp.int32)
        above = (line // nodes) * nodes + above
        reach = jnp.where((column == line) | (column == above), 1.0, 0.0).astype(jnp.bfloat16)
        for level in range(4):
            reach = jnp.minimum(
                jnp.dot(reach, reach, preferred_element_type=jnp.float32), 1.0
            ).astype(jnp.bfloat16)
        reach_ref[...] = reach.astype(jnp.float32)
        value_ref[pl.ds(0, half), :width] = own_ref[:, width:]
        value_ref[pl.ds(half, half), :width] = other_ref[:, width:]
        value_ref[:, width:] = jnp.ones((2 * half, width), jnp.bfloat16)

    scale = 1.0 / math.sqrt(width) * math.log2(math.e) / RAISE
    query = jnp.concatenate(
        [picked_ref[s, :, h * width : (h + 1) * width] for s in range(PAIR) for h in range(heads)],
        axis=0,
    )
    tree = jnp.concatenate([picked_ref[s, :, heads * width :] for s in range(PAIR)], axis=0)
    dims = (((1,), (1,)), ((), ()))
    span = PAIR * nodes
    mask = jnp.zeros((span, span), jnp.float32)
    for k in range(CAP // PAIR):
        block = reach_ref[k * span : (k + 1) * span, k * span : (k + 1) * span]
        mask = jnp.where(step == k, block, mask)
    mask = jnp.concatenate(
        [mask[s * nodes : (s + 1) * nodes] for s in range(PAIR) for h in range(heads)], axis=0
    )
    drafts = lax.dot_general(query, tree[:, :width], dims, preferred_element_type=jnp.float32)
    drafts = jnp.where(mask > 0, drafts * (1.0 / RAISE), NEG)
    peak = jnp.max(drafts, axis=1, keepdims=True)
    drafts = (jnp.exp2((drafts - peak) * scale) * mask).astype(jnp.bfloat16)
    power = tree[:, 2 * width :].astype(jnp.float32) - 10.0
    tree_value = (tree[:, width : 2 * width].astype(jnp.float32) * jnp.exp2(power)).astype(
        jnp.bfloat16
    )
    tree_value = jnp.concatenate([tree_value, jnp.ones((span, width), jnp.bfloat16)], axis=1)
    peaks = [peak]
    sums = [jnp.dot(drafts, tree_value, preferred_element_type=jnp.float32)]
    for k, ref in enumerate((own_ref, other_ref)):
        scores = lax.dot_general(query, ref[:, :width], dims, preferred_element_type=jnp.float32)
        peak = jnp.max(scores, axis=1, keepdims=True)
        weights = jnp.exp2((scores - peak) * scale).astype(jnp.bfloat16)
        peaks.append(peak)
        sums.append(
            jnp.dot(
                weights, value_ref[pl.ds(k * half, half), :], preferred_element_type=jnp.float32
            )
        )
    top = jnp.maximum(jnp.maximum(peaks[0], peaks[1]), peaks[2])
    summed = sum(jnp.exp2((peak - top) * scale) * part for peak, part in zip(peaks, sums))
    attended = (summed[:, :width] / summed[:, width:]).astype(jnp.bfloat16)
    for s in range(PAIR):
        for h in range(heads):
            start = (s * heads + h) * nodes
            out_ref[s, :, h * width : (h + 1) * width] = attended[start : start + nodes]


def attend(slot, parents, picked, own, other):
    nodes = picked.shape[1]
    depth = picked.shape[2]
    width = own.shape[1] // 2
    half = own.shape[0]
    model = depth - 3 * width
    return pl.pallas_call(
        attend_kernel,
        out_shape=jax.ShapeDtypeStruct((CAP, nodes, model), jnp.bfloat16),
        grid=(CAP // PAIR,),
        in_specs=[
            pl.BlockSpec(slot.shape, lambda i: (0, 0)),
            pl.BlockSpec(parents.shape, lambda i: (0, 0)),
            pl.BlockSpec((PAIR, nodes, depth), lambda i: (i, 0, 0)),
            pl.BlockSpec((half, 2 * width), lambda i: (0, 0)),
            pl.BlockSpec((half, 2 * width), lambda i: (0, 0)),
        ],
        out_specs=pl.BlockSpec((PAIR, nodes, model), lambda i: (i, 0, 0)),
        scratch_shapes=[
            pltpu.VMEM((CAP * nodes, CAP * nodes), jnp.float32),
            pltpu.VMEM((2 * half, 2 * width), jnp.bfloat16),
        ],
        compiler_params=pltpu.CompilerParams(vmem_limit_bytes=40 * 1024 * 1024),
        name="attend",
    )(slot, parents, picked, own, other)


def project_kernel(place_ref, every_ref, weight_ref, out_ref, rows_ref, sems):
    lanes, depth = out_ref.shape[0], weight_ref.shape[0]
    requests, nodes = rows_ref.shape[0], rows_ref.shape[1]
    share = requests // lanes
    copies = []
    for r in range(requests):
        copy = pltpu.make_async_copy(every_ref.at[place_ref[0, r]], rows_ref.at[r], sems.at[r])
        copy.start()
        copies.append(copy)
    for lane in range(lanes):
        for copy in copies[lane * share : (lane + 1) * share]:
            copy.wait()
        block = rows_ref[lane * share : (lane + 1) * share].reshape(share * nodes, depth)
        out_ref[lane] = jnp.dot(
            block, weight_ref[...], preferred_element_type=jnp.float32
        ).astype(jnp.bfloat16)


def project(place, every, weight, lanes):
    requests = place.shape[1]
    nodes, depth = every.shape[1], every.shape[2]
    columns = weight.shape[1]
    return pl.pallas_call(
        project_kernel,
        out_shape=jax.ShapeDtypeStruct((lanes, requests // lanes * nodes, columns), jnp.bfloat16),
        grid_spec=pltpu.PrefetchScalarGridSpec(
            num_scalar_prefetch=1,
            grid=(),
            in_specs=[
                pl.BlockSpec(memory_space=pl.ANY),
                pl.BlockSpec(memory_space=pltpu.VMEM),
            ],
            out_specs=pl.BlockSpec(memory_space=pltpu.VMEM),
            scratch_shapes=[
                pltpu.VMEM((requests, nodes, depth), jnp.bfloat16),
                pltpu.SemaphoreType.DMA((requests,)),
            ],
        ),
        compiler_params=pltpu.CompilerParams(vmem_limit_bytes=40 * 1024 * 1024),
        name="project",
    )(place, every, weight)


def local(queries, tree_kv, prefix_kv, request_holder, parents, out_weight):
    group = lax.axis_index("dp")
    lane = lax.axis_index("tensor")
    lanes = lax.axis_size("tensor")
    requests = request_holder.shape[0]
    nodes = queries.shape[1]
    own_half = prefix_kv[0, 0]
    other_half = swapped(own_half, "tensor", 0)
    here = jnp.stack([group, lane // 2]).astype(jnp.int32)
    packed, slot, index, place = pack(here, queries, tree_kv, request_holder)
    packed = lax.all_gather(packed.astype(jnp.float16), "dp", axis=0, tiled=True)
    picked = packed.at[index[0, :CAP]].get(mode="promise_in_bounds").astype(jnp.bfloat16)
    attended = attend(slot, parents, picked, own_half, other_half)
    every = lax.all_gather(attended, "dp", axis=0, tiled=True)
    partial = project(place, every, out_weight, lanes)
    shares = lax.all_to_all(partial, "tensor", 0, 0, tiled=True)
    total = jnp.sum(shares.astype(jnp.float32), axis=0).astype(jnp.bfloat16)
    return total.reshape(requests // lanes, nodes, out_weight.shape[1])


def solution(mesh):
    return jax.shard_map(
        local,
        mesh=mesh,
        in_specs=(
            P("dp", None, "tensor"),
            P("dp", None, None, None),
            P("dp", "tensor", None, None),
            P(),
            P(),
            P("tensor", "dp"),
        ),
        out_specs=P("tensor", None, "dp"),
        check_vma=False,
    )
```

```python
import math

import jax
import jax.numpy as jnp
from jax import lax
from jax.experimental import pallas as pl
from jax.experimental.pallas import tpu as pltpu
from jax.sharding import PartitionSpec as P

CAP = 16
PAIR = 8
NEG = -1e30
RAISE = 2.0**11


def swapped(x, axis, bit):
    return lax.ppermute(x, axis, [(i, i ^ 1 << bit) for i in range(lax.axis_size(axis))])


def exponent(x):
    peak = jnp.max(jnp.abs(x), axis=-1, keepdims=True)
    return jnp.floor(jnp.log2(jnp.clip(peak, 2.0**-100, 2.0**6)))


def pack_kernel(place_ref, queries_ref, tree_ref, holder_ref, packed_ref, slot_ref, index_ref, spot_ref, source_ref):
    group, column = place_ref[0], place_ref[1]
    count, nodes, model = queries_ref.shape
    kv_heads, width = tree_ref.shape[2], tree_ref.shape[3] // 2
    pick = lax.broadcasted_iota(jnp.int32, (nodes, kv_heads, 2 * width), 1) == column
    for r in range(count):
        packed_ref[r, :, :model] = (queries_ref[r].astype(jnp.float32) * RAISE).astype(jnp.bfloat16)
        tree = jnp.sum(jnp.where(pick, tree_ref[r].astype(jnp.float32), 0.0), axis=1)
        packed_ref[r, :, model : model + width] = (tree[:, :width] * RAISE).astype(jnp.bfloat16)
        values = tree[:, width:]
        power = exponent(values)
        packed_ref[r, :, model + width : model + 2 * width] = (
            values * jnp.exp2(10.0 - power)
        ).astype(jnp.bfloat16)
        packed_ref[r, :, model + 2 * width :] = jnp.broadcast_to(power, values.shape).astype(
            jnp.bfloat16
        )
    requests = holder_ref.shape[1]
    line = lax.broadcasted_iota(jnp.int32, (requests, requests), 0)
    lane = lax.broadcasted_iota(jnp.int32, (requests, requests), 1)
    row = holder_ref[...]
    rows = jnp.broadcast_to(row, (requests, requests))
    column = jnp.sum(jnp.where(line == lane, rows, 0), axis=1, keepdims=True)
    before = (column < rows) | ((column == rows) & (line < lane))
    spot = jnp.sum(jnp.where(before, 1, 0), axis=0, keepdims=True)
    before = (rows < column) | ((rows == column) & (lane < line))
    spot_column = jnp.sum(jnp.where(before, 1, 0), axis=1, keepdims=True)
    chips = CAP
    slot_ref[...] = jnp.where(row == group, spot % chips, -1)
    mine = (column == group) & (spot_column % chips == lane)
    index_ref[...] = jnp.sum(jnp.where(mine, line, 0), axis=0, keepdims=True)
    device = 2 * (spot % chips) + spot // chips % 2
    spot_ref[...] = device * (requests // (2 * chips)) + spot // (2 * chips)
    core, chip = group % 2, group // 2
    kept = spot_column == 2 * chips * lane + chips * core + chip
    holder = jnp.sum(jnp.where(kept, column, 0), axis=0, keepdims=True)
    source_ref[...] = jnp.where(holder % 2 == core, 0, chips) + holder // 2


def pack(place, queries, tree, holder):
    count, nodes, model = queries.shape
    width = tree.shape[3] // 2
    requests = holder.shape[0]
    vmem = pl.BlockSpec(memory_space=pltpu.VMEM)
    line = jax.ShapeDtypeStruct((1, requests), jnp.int32)
    return pl.pallas_call(
        pack_kernel,
        out_shape=(
            jax.ShapeDtypeStruct((count, nodes, model + 3 * width), jnp.bfloat16),
            line,
            line,
            line,
            line,
        ),
        grid_spec=pltpu.PrefetchScalarGridSpec(
            num_scalar_prefetch=1, grid=(), in_specs=[vmem] * 3, out_specs=(vmem,) * 5
        ),
        compiler_params=pltpu.CompilerParams(vmem_limit_bytes=40 * 1024 * 1024),
        name="pack",
    )(place, queries, tree, holder.reshape(1, requests))


def attend_kernel(slot_ref, parents_ref, picked_ref, own_ref, other_ref, out_ref, reach_ref, value_ref):
    step = pl.program_id(0)
    nodes = picked_ref.shape[1]
    width = own_ref.shape[1] // 2
    heads = (picked_ref.shape[2] - 3 * width) // width
    half = own_ref.shape[0]
    rows = CAP * nodes

    @pl.when(step == 0)
    def _():
        line = lax.broadcasted_iota(jnp.int32, (rows, rows), 0)
        column = lax.broadcasted_iota(jnp.int32, (rows, rows), 1)
        requests = slot_ref.shape[1]
        taken = lax.broadcasted_iota(jnp.int32, (rows, requests), 0) // nodes == slot_ref[...]
        above = jnp.dot(
            jnp.where(taken, 1.0, 0.0).astype(jnp.bfloat16),
            parents_ref[...].astype(jnp.float32).astype(jnp.bfloat16),
            preferred_element_type=jnp.float32,
        )
        node = lax.broadcasted_iota(jnp.int32, (rows, nodes), 0) % nodes
        own_node = lax.broadcasted_iota(jnp.int32, (rows, nodes), 1) == node
        above = jnp.sum(jnp.where(own_node, above, 0.0), axis=1, keepdims=True).astype(jnp.int32)
        above = (line // nodes) * nodes + above
        reach = jnp.where((column == line) | (column == above), 1.0, 0.0).astype(jnp.bfloat16)
        for level in range(4):
            reach = jnp.minimum(
                jnp.dot(reach, reach, preferred_element_type=jnp.float32), 1.0
            ).astype(jnp.bfloat16)
        reach_ref[...] = reach.astype(jnp.float32)
        value_ref[pl.ds(0, half), :width] = own_ref[:, width:]
        value_ref[pl.ds(half, half), :width] = other_ref[:, width:]
        value_ref[:, width:] = jnp.ones((2 * half, width), jnp.bfloat16)

    scale = 1.0 / math.sqrt(width) * math.log2(math.e) / RAISE
    query = jnp.concatenate(
        [picked_ref[s, :, h * width : (h + 1) * width] for s in range(PAIR) for h in range(heads)],
        axis=0,
    )
    tree = jnp.concatenate([picked_ref[s, :, heads * width :] for s in range(PAIR)], axis=0)
    dims = (((1,), (1,)), ((), ()))
    span = PAIR * nodes
    mask = jnp.zeros((span, span), jnp.float32)
    for k in range(CAP // PAIR):
        block = reach_ref[k * span : (k + 1) * span, k * span : (k + 1) * span]
        mask = jnp.where(step == k, block, mask)
    mask = jnp.concatenate(
        [mask[s * nodes : (s + 1) * nodes] for s in range(PAIR) for h in range(heads)], axis=0
    )
    drafts = lax.dot_general(query, tree[:, :width], dims, preferred_element_type=jnp.float32)
    drafts = jnp.where(mask > 0, drafts * (1.0 / RAISE), NEG)
    peak = jnp.max(drafts, axis=1, keepdims=True)
    drafts = (jnp.exp2((drafts - peak) * scale) * mask).astype(jnp.bfloat16)
    power = tree[:, 2 * width :].astype(jnp.float32) - 10.0
    tree_value = (tree[:, width : 2 * width].astype(jnp.float32) * jnp.exp2(power)).astype(
        jnp.bfloat16
    )
    tree_value = jnp.concatenate([tree_value, jnp.ones((span, width), jnp.bfloat16)], axis=1)
    peaks = [peak]
    sums = [jnp.dot(drafts, tree_value, preferred_element_type=jnp.float32)]
    for k, ref in enumerate((own_ref, other_ref)):
        scores = lax.dot_general(query, ref[:, :width], dims, preferred_element_type=jnp.float32)
        peak = jnp.max(scores, axis=1, keepdims=True)
        weights = jnp.exp2((scores - peak) * scale).astype(jnp.bfloat16)
        peaks.append(peak)
        sums.append(
            jnp.dot(
                weights, value_ref[pl.ds(k * half, half), :], preferred_element_type=jnp.float32
            )
        )
    top = jnp.maximum(jnp.maximum(peaks[0], peaks[1]), peaks[2])
    summed = sum(jnp.exp2((peak - top) * scale) * part for peak, part in zip(peaks, sums))
    attended = (summed[:, :width] / summed[:, width:]).astype(jnp.bfloat16)
    for s in range(PAIR):
        for h in range(heads):
            start = (s * heads + h) * nodes
            out_ref[s, :, h * width : (h + 1) * width] = attended[start : start + nodes]


def attend(slot, parents, picked, own, other):
    nodes = picked.shape[1]
    depth = picked.shape[2]
    width = own.shape[1] // 2
    half = own.shape[0]
    model = depth - 3 * width
    return pl.pallas_call(
        attend_kernel,
        out_shape=jax.ShapeDtypeStruct((CAP, nodes, model), jnp.bfloat16),
        grid=(CAP // PAIR,),
        in_specs=[
            pl.BlockSpec(slot.shape, lambda i: (0, 0)),
            pl.BlockSpec(parents.shape, lambda i: (0, 0)),
            pl.BlockSpec((PAIR, nodes, depth), lambda i: (i, 0, 0)),
            pl.BlockSpec((half, 2 * width), lambda i: (0, 0)),
            pl.BlockSpec((half, 2 * width), lambda i: (0, 0)),
        ],
        out_specs=pl.BlockSpec((PAIR, nodes, model), lambda i: (i, 0, 0)),
        scratch_shapes=[
            pltpu.VMEM((CAP * nodes, CAP * nodes), jnp.float32),
            pltpu.VMEM((2 * half, 2 * width), jnp.bfloat16),
        ],
        compiler_params=pltpu.CompilerParams(vmem_limit_bytes=40 * 1024 * 1024),
        name="attend",
    )(slot, parents, picked, own, other)


def settle_kernel(source_ref, own_ref, other_ref, out_ref):
    count, model = out_ref.shape[0], own_ref.shape[2]
    chips = own_ref.shape[0]
    for k in range(count):
        source = source_ref[0, k]
        chip = source % chips
        rows = jnp.where(
            source < chips, own_ref[chip].astype(jnp.float32), other_ref[chip].astype(jnp.float32)
        )
        power = exponent(rows)
        out_ref[k, :, :model] = (rows * jnp.exp2(10.0 - power)).astype(jnp.bfloat16)
        width = out_ref.shape[2] - model
        out_ref[k, :, model:] = jnp.broadcast_to(power, (rows.shape[0], width)).astype(jnp.bfloat16)


def settle(source, own, other, count):
    nodes, model = own.shape[1:]
    vmem = pl.BlockSpec(memory_space=pltpu.VMEM)
    return pl.pallas_call(
        settle_kernel,
        out_shape=jax.ShapeDtypeStruct((count, nodes, model + 128), jnp.bfloat16),
        grid_spec=pltpu.PrefetchScalarGridSpec(
            num_scalar_prefetch=1, grid=(), in_specs=[vmem] * 2, out_specs=vmem
        ),
        compiler_params=pltpu.CompilerParams(vmem_limit_bytes=40 * 1024 * 1024),
        name="settle",
    )(source, own, other)


def project_kernel(spot_ref, every_ref, weight_ref, out_ref):
    lanes, depth = out_ref.shape[0], weight_ref.shape[0]
    share = every_ref.shape[0] // lanes
    for lane in range(lanes):
        block = jnp.concatenate(
            [every_ref[spot_ref[0, lane * share + r]] for r in range(share)], axis=0
        )
        power = block[:, depth : depth + 1].astype(jnp.float32) - 10.0
        product = jnp.dot(
            block[:, :depth], weight_ref[...], preferred_element_type=jnp.float32
        )
        out_ref[lane] = (product * jnp.exp2(power)).astype(jnp.bfloat16)


def project(spot, every, weight, lanes):
    requests, nodes = every.shape[:2]
    columns = weight.shape[1]
    vmem = pl.BlockSpec(memory_space=pltpu.VMEM)
    return pl.pallas_call(
        project_kernel,
        out_shape=jax.ShapeDtypeStruct((lanes, requests // lanes * nodes, columns), jnp.bfloat16),
        grid_spec=pltpu.PrefetchScalarGridSpec(
            num_scalar_prefetch=1, grid=(), in_specs=[vmem] * 2, out_specs=vmem
        ),
        compiler_params=pltpu.CompilerParams(vmem_limit_bytes=40 * 1024 * 1024),
        name="project",
    )(spot, every, weight)


def local(queries, tree_kv, prefix_kv, request_holder, parents, out_weight):
    group = lax.axis_index("dp")
    lane = lax.axis_index("tensor")
    lanes = lax.axis_size("tensor")
    requests = request_holder.shape[0]
    nodes = queries.shape[1]
    own_half = prefix_kv[0, 0]
    other_half = swapped(own_half, "tensor", 0)
    here = jnp.stack([group, lane // 2]).astype(jnp.int32)
    packed, slot, index, spot, source = pack(here, queries, tree_kv, request_holder)
    packed = lax.all_gather(packed.astype(jnp.float16), "dp", axis=0, tiled=True)
    picked = packed.at[index[0, :CAP]].get(mode="promise_in_bounds").astype(jnp.bfloat16)
    attended = attend(slot, parents, picked, own_half, other_half)
    groups = lax.axis_size("dp")
    along = [[i for i in range(groups) if i % 2 == core] for core in range(2)]
    spread = lax.all_to_all(attended, "dp", 0, 0, axis_index_groups=along, tiled=True)
    settled = settle(source, spread, swapped(spread, "dp", 0), requests // groups)
    every = lax.all_gather(settled.astype(jnp.float16), "dp", axis=0, tiled=True)
    partial = project(spot, every.astype(jnp.bfloat16), out_weight, lanes)
    shares = lax.all_to_all(partial, "tensor", 0, 0, tiled=True)
    total = jnp.sum(shares.astype(jnp.float32), axis=0).astype(jnp.bfloat16)
    return total.reshape(requests // lanes, nodes, out_weight.shape[1])


def solution(mesh):
    return jax.shard_map(
        local,
        mesh=mesh,
        in_specs=(
            P("dp", None, "tensor"),
            P("dp", None, None, None),
            P("dp", "tensor", None, None),
            P(),
            P(),
            P("tensor", "dp"),
        ),
        out_specs=P("tensor", None, "dp"),
        check_vma=False,
    )
```

```python
import math

import jax
import jax.numpy as jnp
from jax import lax
from jax.experimental import pallas as pl
from jax.experimental.pallas import tpu as pltpu
from jax.sharding import PartitionSpec as P

CAP = 16
PAIR = 8
NEG = -1e30
LIFT = 2.0**59


def swapped(x, axis, bit):
    return lax.ppermute(x, axis, [(i, i ^ 1 << bit) for i in range(lax.axis_size(axis))])


def encode(x):
    root = jnp.sqrt(jnp.sqrt(jnp.abs(x) * LIFT))
    return jnp.where(x < 0, -root, root)


def decode(x):
    x = x.astype(jnp.float32)
    return ((x * jnp.abs(x)) * ((x * (1.0 / LIFT)) * x)).astype(jnp.bfloat16)


def pack_kernel(
    place_ref,
    queries_hbm,
    tree_hbm,
    holder_hbm,
    packed_ref,
    slot_ref,
    index_ref,
    spot_ref,
    source_ref,
    queries_ref,
    tree_ref,
    holder_ref,
    sems,
):
    group, column = place_ref[0], place_ref[1]
    count, nodes, model = queries_ref.shape
    kv_heads, width = tree_ref.shape[2], tree_ref.shape[3] // 2
    copies = [
        pltpu.make_async_copy(source, target, sems.at[k])
        for k, (source, target) in enumerate(
            ((holder_hbm, holder_ref), (queries_hbm, queries_ref), (tree_hbm, tree_ref))
        )
    ]
    for copy in copies:
        copy.start()
    copies[0].wait()
    plan(group, holder_ref, slot_ref, index_ref, spot_ref, source_ref)
    copies[1].wait()
    for r in range(count):
        packed_ref[r, :, :model] = encode(queries_ref[r].astype(jnp.float32))
    copies[2].wait()
    pick = lax.broadcasted_iota(jnp.int32, (nodes, kv_heads, 2 * width), 1) == column
    for r in range(count):
        tree = jnp.sum(jnp.where(pick, tree_ref[r].astype(jnp.float32), 0.0), axis=1)
        packed_ref[r, :, model:] = encode(tree)


def plan(group, holder_ref, slot_ref, index_ref, spot_ref, source_ref):
    requests = holder_ref.shape[1]
    line = lax.broadcasted_iota(jnp.int32, (requests, requests), 0)
    lane = lax.broadcasted_iota(jnp.int32, (requests, requests), 1)
    row = holder_ref[...]
    rows = jnp.broadcast_to(row, (requests, requests))
    column = jnp.sum(jnp.where(line == lane, rows, 0), axis=1, keepdims=True)
    before = (column < rows) | ((column == rows) & (line < lane))
    spot = jnp.sum(jnp.where(before, 1, 0), axis=0, keepdims=True)
    before = (rows < column) | ((rows == column) & (lane < line))
    spot_column = jnp.sum(jnp.where(before, 1, 0), axis=1, keepdims=True)
    chips = CAP
    slot_ref[...] = jnp.where(row == group, spot % chips, -1)
    mine = (column == group) & (spot_column % chips == lane)
    index_ref[...] = jnp.sum(jnp.where(mine, line, 0), axis=0, keepdims=True)
    device = 2 * (spot % chips) + spot // chips % 2
    spot_ref[...] = device * (requests // (2 * chips)) + spot // (2 * chips)
    core, chip = group % 2, group // 2
    kept = spot_column == 2 * chips * lane + chips * core + chip
    holder = jnp.sum(jnp.where(kept, column, 0), axis=0, keepdims=True)
    source_ref[...] = jnp.where(holder % 2 == core, 0, chips) + holder // 2


def pack(place, queries, tree, holder):
    count, nodes, model = queries.shape
    width = tree.shape[3] // 2
    requests = holder.shape[0]
    vmem = pl.BlockSpec(memory_space=pltpu.VMEM)
    hbm = pl.BlockSpec(memory_space=pltpu.HBM)
    line = jax.ShapeDtypeStruct((1, requests), jnp.int32)
    holder = holder.reshape(1, requests)
    return pl.pallas_call(
        pack_kernel,
        out_shape=(
            jax.ShapeDtypeStruct((count, nodes, model + 2 * width), jnp.float32),
            line,
            line,
            line,
            line,
        ),
        grid_spec=pltpu.PrefetchScalarGridSpec(
            num_scalar_prefetch=1,
            grid=(),
            in_specs=[hbm] * 3,
            out_specs=(vmem,) * 5,
            scratch_shapes=[
                pltpu.VMEM(queries.shape, queries.dtype),
                pltpu.VMEM(tree.shape, tree.dtype),
                pltpu.VMEM(holder.shape, holder.dtype),
                pltpu.SemaphoreType.DMA((3,)),
            ],
        ),
        compiler_params=pltpu.CompilerParams(vmem_limit_bytes=60 * 1024 * 1024),
        name="pack",
    )(place, queries, tree, holder)


def attend_kernel(index_ref, slot_ref, parents_ref, packed_ref, own_ref, other_ref, out_ref, reach_ref, value_ref):
    step = pl.program_id(0)
    nodes = packed_ref.shape[1]
    width = own_ref.shape[1] // 2
    heads = (packed_ref.shape[2] - 2 * width) // width
    half = own_ref.shape[0]
    rows = CAP * nodes

    @pl.when(step == 0)
    def _():
        line = lax.broadcasted_iota(jnp.int32, (rows, rows), 0)
        column = lax.broadcasted_iota(jnp.int32, (rows, rows), 1)
        requests = slot_ref.shape[1]
        taken = lax.broadcasted_iota(jnp.int32, (rows, requests), 0) // nodes == slot_ref[...]
        above = jnp.dot(
            jnp.where(taken, 1.0, 0.0).astype(jnp.bfloat16),
            parents_ref[...].astype(jnp.float32).astype(jnp.bfloat16),
            preferred_element_type=jnp.float32,
        )
        node = lax.broadcasted_iota(jnp.int32, (rows, nodes), 0) % nodes
        own_node = lax.broadcasted_iota(jnp.int32, (rows, nodes), 1) == node
        above = jnp.sum(jnp.where(own_node, above, 0.0), axis=1, keepdims=True).astype(jnp.int32)
        above = (line // nodes) * nodes + above
        reach = jnp.where((column == line) | (column == above), 1.0, 0.0).astype(jnp.bfloat16)
        for level in range(4):
            reach = jnp.minimum(
                jnp.dot(reach, reach, preferred_element_type=jnp.float32), 1.0
            ).astype(jnp.bfloat16)
        reach_ref[...] = reach.astype(jnp.float32)
        value_ref[pl.ds(0, half), :width] = own_ref[:, width:]
        value_ref[pl.ds(half, half), :width] = other_ref[:, width:]
        value_ref[:, width:] = jnp.ones((2 * half, width), jnp.bfloat16)

    scale = 1.0 / math.sqrt(width) * math.log2(math.e)
    places = [index_ref[0, step * PAIR + s] for s in range(PAIR)]
    query = jnp.concatenate(
        [packed_ref[r, :, h * width : (h + 1) * width] for r in places for h in range(heads)],
        axis=0,
    )
    tree = jnp.concatenate([packed_ref[r, :, heads * width :] for r in places], axis=0)
    dims = (((1,), (1,)), ((), ()))
    span = PAIR * nodes
    mask = jnp.zeros((span, span), jnp.float32)
    for k in range(CAP // PAIR):
        block = reach_ref[k * span : (k + 1) * span, k * span : (k + 1) * span]
        mask = jnp.where(step == k, block, mask)
    mask = jnp.concatenate(
        [mask[s * nodes : (s + 1) * nodes] for s in range(PAIR) for h in range(heads)], axis=0
    )
    drafts = lax.dot_general(query, tree[:, :width], dims, preferred_element_type=jnp.float32)
    drafts = jnp.where(mask > 0, drafts, NEG)
    peak = jnp.max(drafts, axis=1, keepdims=True)
    drafts = (jnp.exp2((drafts - peak) * scale) * mask).astype(jnp.bfloat16)
    tree_value = jnp.concatenate([tree[:, width:], jnp.ones((span, width), jnp.bfloat16)], axis=1)
    peaks = [peak]
    sums = [jnp.dot(drafts, tree_value, preferred_element_type=jnp.float32)]
    for k, ref in enumerate((own_ref, other_ref)):
        scores = lax.dot_general(query, ref[:, :width], dims, preferred_element_type=jnp.float32)
        peak = jnp.max(scores, axis=1, keepdims=True)
        weights = jnp.exp2((scores - peak) * scale).astype(jnp.bfloat16)
        peaks.append(peak)
        sums.append(
            jnp.dot(
                weights, value_ref[pl.ds(k * half, half), :], preferred_element_type=jnp.float32
            )
        )
    top = jnp.maximum(jnp.maximum(peaks[0], peaks[1]), peaks[2])
    summed = sum(jnp.exp2((peak - top) * scale) * part for peak, part in zip(peaks, sums))
    attended = (summed[:, :width] / summed[:, width:]).astype(jnp.bfloat16)
    for s in range(PAIR):
        for h in range(heads):
            start = (s * heads + h) * nodes
            out_ref[s, :, h * width : (h + 1) * width] = attended[start : start + nodes]


def attend(index, slot, parents, packed, own, other):
    nodes, depth = packed.shape[1:]
    width = own.shape[1] // 2
    half = own.shape[0]
    model = depth - 2 * width
    return pl.pallas_call(
        attend_kernel,
        out_shape=jax.ShapeDtypeStruct((CAP, nodes, model), jnp.bfloat16),
        grid_spec=pltpu.PrefetchScalarGridSpec(
            num_scalar_prefetch=1,
            grid=(CAP // PAIR,),
            in_specs=[pl.BlockSpec(memory_space=pltpu.VMEM)] * 5,
            out_specs=pl.BlockSpec((PAIR, nodes, model), lambda i, index: (i, 0, 0)),
            scratch_shapes=[
                pltpu.VMEM((CAP * nodes, CAP * nodes), jnp.float32),
                pltpu.VMEM((2 * half, 2 * width), jnp.bfloat16),
            ],
        ),
        compiler_params=pltpu.CompilerParams(vmem_limit_bytes=28 * 1024 * 1024),
        name="attend",
    )(index, slot, parents, packed, own, other)


def settle_kernel(source_ref, own_ref, other_ref, out_ref):
    chips = own_ref.shape[0]
    for k in range(out_ref.shape[0]):
        source = source_ref[0, k]
        chip = source % chips
        out_ref[k] = encode(
            jnp.where(
                source < chips,
                own_ref[chip].astype(jnp.float32),
                other_ref[chip].astype(jnp.float32),
            )
        )


def settle(source, own, other, count):
    nodes, model = own.shape[1:]
    vmem = pl.BlockSpec(memory_space=pltpu.VMEM)
    return pl.pallas_call(
        settle_kernel,
        out_shape=jax.ShapeDtypeStruct((count, nodes, model), jnp.float32),
        grid_spec=pltpu.PrefetchScalarGridSpec(
            num_scalar_prefetch=1, grid=(), in_specs=[vmem] * 2, out_specs=vmem
        ),
        compiler_params=pltpu.CompilerParams(vmem_limit_bytes=40 * 1024 * 1024),
        name="settle",
    )(source, own, other)


def project_kernel(spot_ref, every_ref, weight_ref, out_ref):
    lanes = out_ref.shape[0]
    share = every_ref.shape[0] // lanes
    for lane in range(lanes):
        block = jnp.concatenate(
            [every_ref[spot_ref[0, lane * share + r]] for r in range(share)], axis=0
        )
        out_ref[lane] = jnp.dot(
            block, weight_ref[...], preferred_element_type=jnp.float32
        ).astype(jnp.bfloat16)


def project(spot, every, weight, lanes):
    requests, nodes = every.shape[:2]
    columns = weight.shape[1]
    vmem = pl.BlockSpec(memory_space=pltpu.VMEM)
    return pl.pallas_call(
        project_kernel,
        out_shape=jax.ShapeDtypeStruct((lanes, requests // lanes * nodes, columns), jnp.bfloat16),
        grid_spec=pltpu.PrefetchScalarGridSpec(
            num_scalar_prefetch=1, grid=(), in_specs=[vmem] * 2, out_specs=vmem
        ),
        compiler_params=pltpu.CompilerParams(vmem_limit_bytes=40 * 1024 * 1024),
        name="project",
    )(spot, every, weight)


def local(queries, tree_kv, prefix_kv, request_holder, parents, out_weight):
    group = lax.axis_index("dp")
    lane = lax.axis_index("tensor")
    lanes = lax.axis_size("tensor")
    requests = request_holder.shape[0]
    nodes = queries.shape[1]
    own_half = prefix_kv[0, 0]
    other_half = swapped(own_half, "tensor", 0)
    here = jnp.stack([group, lane // 2]).astype(jnp.int32)
    packed, slot, index, spot, source = pack(here, queries, tree_kv, request_holder)
    packed = lax.all_gather(packed.astype(jnp.float16), "dp", axis=0, tiled=True)
    packed = decode(packed)
    attended = attend(index, slot, parents, packed, own_half, other_half)
    groups = lax.axis_size("dp")
    along = [[i for i in range(groups) if i % 2 == core] for core in range(2)]
    spread = lax.all_to_all(attended, "dp", 0, 0, axis_index_groups=along, tiled=True)
    settled = settle(source, spread, swapped(spread, "dp", 0), requests // groups)
    every = lax.all_gather(settled.astype(jnp.float16), "dp", axis=0, tiled=True)
    every = decode(every)
    partial = project(spot, every, out_weight, lanes)
    shares = lax.all_to_all(partial, "tensor", 0, 0, tiled=True)
    total = jnp.sum(shares.astype(jnp.float32), axis=0).astype(jnp.bfloat16)
    return total.reshape(requests // lanes, nodes, out_weight.shape[1])


def solution(mesh):
    return jax.shard_map(
        local,
        mesh=mesh,
        in_specs=(
            P("dp", None, "tensor"),
            P("dp", None, None, None),
            P("dp", "tensor", None, None),
            P(),
            P(),
            P("tensor", "dp"),
        ),
        out_specs=P("tensor", None, "dp"),
        check_vma=False,
    )
```

```python
import functools
import math

import jax
import jax.numpy as jnp
from jax import lax
from jax.experimental import pallas as pl
from jax.experimental.pallas import tpu as pltpu
from jax.sharding import PartitionSpec as P

CAP = 16
PAIR = 16
BLOCK = 8
ROWS = (6, 7, 8, 16)
NEG = -1e30
LIFT = 2.0**59


def swapped(x, axis, bit):
    return lax.ppermute(x, axis, [(i, i ^ 1 << bit) for i in range(lax.axis_size(axis))])


def encode(x):
    root = jnp.sqrt(jnp.sqrt(jnp.abs(x) * LIFT))
    return jnp.where(x < 0, -root, root)


def decode(x):
    x = x.astype(jnp.float32)
    return ((x * jnp.abs(x)) * ((x * (1.0 / LIFT)) * x)).astype(jnp.bfloat16)


def pack_kernel(
    queries_ref, tree_ref, holder_ref, packed_ref, slot_ref, index_ref, spot_ref, source_ref, most_ref
):
    group, column = lax.axis_index("dp"), lax.axis_index("tensor") // 2
    count, nodes, model = queries_ref.shape
    kv_heads, width = tree_ref.shape[2], tree_ref.shape[3] // 2
    pick = lax.broadcasted_iota(jnp.int32, (nodes, kv_heads, 2 * width), 1) == column
    for r in range(count):
        packed_ref[r, :, :model] = encode(queries_ref[r].astype(jnp.float32))
        tree = jnp.sum(jnp.where(pick, tree_ref[r].astype(jnp.float32), 0.0), axis=1)
        packed_ref[r, :, model:] = encode(tree)
    requests = holder_ref.shape[1]
    line = lax.broadcasted_iota(jnp.int32, (requests, requests), 0)
    lane = lax.broadcasted_iota(jnp.int32, (requests, requests), 1)
    row = holder_ref[...]
    rows = jnp.broadcast_to(row, (requests, requests))
    column = jnp.sum(jnp.where(line == lane, rows, 0), axis=1, keepdims=True)

    def counted(chosen, axis):
        return jnp.sum(jnp.where(chosen, 1, 0), axis=axis, keepdims=True)

    same, earlier, later = column == rows, line < lane, lane < line
    block = (column >> 3) == (rows >> 3)
    rank, rank_line = counted(same & earlier, 0), counted(same & later, 1)
    place = counted(block & ((column < rows) | (same & earlier)), 0)
    place_line = counted(block & ((rows < column) | (same & later)), 1)
    slot = (place & 7) * 2 + (rank >> 3)
    slot_line = (place_line & 7) * 2 + (rank_line >> 3)
    slot_ref[...] = jnp.where(row == group, slot, -1)
    mine = (column == group) & (slot_line == lane)
    index_ref[...] = jnp.sum(jnp.where(mine, line, 0), axis=0, keepdims=True)
    device = (row >> 3) * BLOCK + (place & 7)
    for k, height in enumerate(ROWS):
        spot_ref[k : k + 1, :] = device * height + (place >> 3)
    kept = ((column >> 3) == (group >> 3)) & (place_line == BLOCK * lane + (group & 7))
    source = (column & 7) * 2 + (rank_line >> 3)
    source_ref[...] = jnp.sum(jnp.where(kept, source, 0), axis=0, keepdims=True)
    most = jnp.max(place, axis=1, keepdims=True) // BLOCK + 1
    choice = sum(jnp.where(most > height, 1, 0) for height in ROWS[:-1])
    most_ref[...] = jnp.broadcast_to(choice, most_ref.shape)


def pack(queries, tree, holder):
    count, nodes, model = queries.shape
    width = tree.shape[3] // 2
    requests = holder.shape[0]
    vmem = pl.BlockSpec(memory_space=pltpu.VMEM)
    line = jax.ShapeDtypeStruct((1, requests), jnp.int32)
    return pl.pallas_call(
        pack_kernel,
        out_shape=(
            jax.ShapeDtypeStruct((count, nodes, model + 2 * width), jnp.float32),
            line,
            line,
            jax.ShapeDtypeStruct((len(ROWS), requests), jnp.int32),
            line,
            line,
        ),
        in_specs=[vmem] * 3,
        out_specs=(vmem,) * 6,
        compiler_params=pltpu.CompilerParams(vmem_limit_bytes=40 * 1024 * 1024),
        name="pack",
    )(queries, tree, holder.reshape(1, requests))


def attend_kernel(slot_ref, parents_ref, picked_ref, own_ref, other_ref, out_ref, reach_ref, value_ref):
    step = pl.program_id(0)
    nodes = picked_ref.shape[1]
    width = own_ref.shape[1] // 2
    heads = (picked_ref.shape[2] - 2 * width) // width
    half = own_ref.shape[0]
    rows = CAP * nodes

    @pl.when(step == 0)
    def _():
        line = lax.broadcasted_iota(jnp.int32, (rows, rows), 0)
        column = lax.broadcasted_iota(jnp.int32, (rows, rows), 1)
        requests = slot_ref.shape[1]
        taken = lax.broadcasted_iota(jnp.int32, (rows, requests), 0) // nodes == slot_ref[...]
        above = jnp.dot(
            jnp.where(taken, 1.0, 0.0).astype(jnp.bfloat16),
            parents_ref[...].astype(jnp.float32).astype(jnp.bfloat16),
            preferred_element_type=jnp.float32,
        )
        node = lax.broadcasted_iota(jnp.int32, (rows, nodes), 0) % nodes
        own_node = lax.broadcasted_iota(jnp.int32, (rows, nodes), 1) == node
        above = jnp.sum(jnp.where(own_node, above, 0.0), axis=1, keepdims=True).astype(jnp.int32)
        above = (line // nodes) * nodes + above
        reach = jnp.where((column == line) | (column == above), 1.0, 0.0).astype(jnp.bfloat16)
        for level in range(4):
            reach = jnp.minimum(
                jnp.dot(reach, reach, preferred_element_type=jnp.float32), 1.0
            ).astype(jnp.bfloat16)
        reach_ref[...] = reach.astype(jnp.float32)
        value_ref[pl.ds(0, half), :width] = own_ref[:, width:]
        value_ref[pl.ds(half, half), :width] = other_ref[:, width:]
        value_ref[:, width:] = jnp.ones((2 * half, width), jnp.bfloat16)

    scale = 1.0 / math.sqrt(width) * math.log2(math.e)
    query = jnp.concatenate(
        [picked_ref[s, :, h * width : (h + 1) * width] for s in range(PAIR) for h in range(heads)],
        axis=0,
    )
    tree = jnp.concatenate([picked_ref[s, :, heads * width :] for s in range(PAIR)], axis=0)
    dims = (((1,), (1,)), ((), ()))
    span = PAIR * nodes
    mask = jnp.zeros((span, span), jnp.float32)
    for k in range(CAP // PAIR):
        block = reach_ref[k * span : (k + 1) * span, k * span : (k + 1) * span]
        mask = jnp.where(step == k, block, mask)
    mask = jnp.concatenate(
        [mask[s * nodes : (s + 1) * nodes] for s in range(PAIR) for h in range(heads)], axis=0
    )
    drafts = lax.dot_general(query, tree[:, :width], dims, preferred_element_type=jnp.float32)
    drafts = jnp.where(mask > 0, drafts, NEG)
    peak = jnp.max(drafts, axis=1, keepdims=True)
    drafts = (jnp.exp2((drafts - peak) * scale) * mask).astype(jnp.bfloat16)
    tree_value = jnp.concatenate([tree[:, width:], jnp.ones((span, width), jnp.bfloat16)], axis=1)
    peaks = [peak]
    sums = [jnp.dot(drafts, tree_value, preferred_element_type=jnp.float32)]
    for k, ref in enumerate((own_ref, other_ref)):
        scores = lax.dot_general(query, ref[:, :width], dims, preferred_element_type=jnp.float32)
        peak = jnp.max(scores, axis=1, keepdims=True)
        weights = jnp.exp2((scores - peak) * scale).astype(jnp.bfloat16)
        peaks.append(peak)
        sums.append(
            jnp.dot(
                weights, value_ref[pl.ds(k * half, half), :], preferred_element_type=jnp.float32
            )
        )
    top = jnp.maximum(jnp.maximum(peaks[0], peaks[1]), peaks[2])
    summed = sum(jnp.exp2((peak - top) * scale) * part for peak, part in zip(peaks, sums))
    attended = (summed[:, :width] / summed[:, width:]).astype(jnp.bfloat16)
    for s in range(PAIR):
        for h in range(heads):
            start = (s * heads + h) * nodes
            out_ref[s, :, h * width : (h + 1) * width] = attended[start : start + nodes]


def attend(slot, parents, picked, own, other):
    nodes, depth = picked.shape[1:]
    width = own.shape[1] // 2
    half = own.shape[0]
    model = depth - 2 * width
    return pl.pallas_call(
        attend_kernel,
        out_shape=jax.ShapeDtypeStruct((CAP, nodes, model), jnp.bfloat16),
        grid=(CAP // PAIR,),
        in_specs=[
            pl.BlockSpec(slot.shape, lambda i: (0, 0)),
            pl.BlockSpec(parents.shape, lambda i: (0, 0)),
            pl.BlockSpec((PAIR, nodes, depth), lambda i: (i, 0, 0)),
            pl.BlockSpec((half, 2 * width), lambda i: (0, 0)),
            pl.BlockSpec((half, 2 * width), lambda i: (0, 0)),
        ],
        out_specs=pl.BlockSpec((PAIR, nodes, model), lambda i: (i, 0, 0)),
        scratch_shapes=[
            pltpu.VMEM((CAP * nodes, CAP * nodes), jnp.float32),
            pltpu.VMEM((2 * half, 2 * width), jnp.bfloat16),
        ],
        compiler_params=pltpu.CompilerParams(vmem_limit_bytes=40 * 1024 * 1024),
        name="attend",
    )(slot, parents, picked, own, other)


def settle_kernel(source_ref, spread_ref, out_ref):
    for k in range(out_ref.shape[0]):
        out_ref[k] = encode(spread_ref[source_ref[0, k]].astype(jnp.float32))


def settle(source, spread, count):
    vmem = pl.BlockSpec(memory_space=pltpu.VMEM)
    return pl.pallas_call(
        settle_kernel,
        out_shape=jax.ShapeDtypeStruct((count, *spread.shape[1:]), jnp.float32),
        grid_spec=pltpu.PrefetchScalarGridSpec(
            num_scalar_prefetch=1, grid=(), in_specs=[vmem], out_specs=vmem
        ),
        compiler_params=pltpu.CompilerParams(vmem_limit_bytes=40 * 1024 * 1024),
        name="settle",
    )(source, spread)


def project_kernel(choice, spot_ref, every_ref, weight_ref, out_ref):
    lanes = out_ref.shape[0]
    share = spot_ref.shape[1] // lanes
    for lane in range(lanes):
        block = jnp.concatenate(
            [every_ref[spot_ref[choice, lane * share + r]] for r in range(share)], axis=0
        )
        out_ref[lane] = jnp.dot(
            block, weight_ref[...], preferred_element_type=jnp.float32
        ).astype(jnp.bfloat16)


def project(choice, spot, every, weight, lanes):
    requests, nodes = spot.shape[1], every.shape[1]
    columns = weight.shape[1]
    vmem = pl.BlockSpec(memory_space=pltpu.VMEM)
    return pl.pallas_call(
        functools.partial(project_kernel, choice),
        out_shape=jax.ShapeDtypeStruct((lanes, requests // lanes * nodes, columns), jnp.bfloat16),
        grid_spec=pltpu.PrefetchScalarGridSpec(
            num_scalar_prefetch=1, grid=(), in_specs=[vmem] * 2, out_specs=vmem
        ),
        compiler_params=pltpu.CompilerParams(vmem_limit_bytes=40 * 1024 * 1024),
        name="project",
    )(spot, every, weight)


def share_rows(choice, lanes, source, spread, spot, weight):
    settled = settle(source, spread, ROWS[choice])
    every = lax.all_gather(settled.astype(jnp.float16), "dp", axis=0, tiled=True)
    return project(choice, spot, decode(every), weight, lanes)


def local(queries, tree_kv, prefix_kv, request_holder, parents, out_weight):
    lanes = lax.axis_size("tensor")
    groups = lax.axis_size("dp")
    requests = request_holder.shape[0]
    nodes = queries.shape[1]
    own_half = prefix_kv[0, 0]
    other_half = swapped(own_half, "tensor", 0)
    packed, slot, index, spot, source, most = pack(queries, tree_kv, request_holder)
    packed = lax.all_gather(packed.astype(jnp.float16), "dp", axis=0, tiled=True)
    picked = decode(packed.at[index[0, :CAP]].get(mode="promise_in_bounds"))
    attended = attend(slot, parents, picked, own_half, other_half)
    blocks = [list(range(i, i + BLOCK)) for i in range(0, groups, BLOCK)]
    spread = lax.all_to_all(attended, "dp", 0, 0, axis_index_groups=blocks, tiled=True)
    partial = lax.switch(
        most[0, 0],
        [functools.partial(share_rows, choice, lanes) for choice in range(len(ROWS))],
        source,
        spread,
        spot,
        out_weight,
    )
    shares = lax.all_to_all(partial, "tensor", 0, 0, tiled=True)
    total = jnp.sum(shares.astype(jnp.float32), axis=0).astype(jnp.bfloat16)
    return total.reshape(requests // lanes, nodes, out_weight.shape[1])


def solution(mesh):
    return jax.shard_map(
        local,
        mesh=mesh,
        in_specs=(
            P("dp", None, "tensor"),
            P("dp", None, None, None),
            P("dp", "tensor", None, None),
            P(),
            P(),
            P("tensor", "dp"),
        ),
        out_specs=P("tensor", None, "dp"),
        check_vma=False,
    )
```

```python
import functools
import math

import jax
import jax.numpy as jnp
from jax import lax
from jax.experimental import pallas as pl
from jax.experimental.pallas import tpu as pltpu
from jax.sharding import PartitionSpec as P

CAP = 16
PAIR = 16
BLOCK = 8
ROWS = (6, 7, 8, 16)
NEG = -1e30
LIFT = 2.0**59


def swapped(x, axis, bit):
    return lax.ppermute(x, axis, [(i, i ^ 1 << bit) for i in range(lax.axis_size(axis))])


def encode(x):
    root = jnp.sqrt(jnp.sqrt(jnp.abs(x) * LIFT))
    return jnp.where(x < 0, -root, root)


def decode(x):
    x = x.astype(jnp.float32)
    return ((x * jnp.abs(x)) * ((x * (1.0 / LIFT)) * x)).astype(jnp.bfloat16)


def pack_kernel(
    queries_ref, tree_ref, holder_ref, packed_ref, slot_ref, index_ref, spot_ref, source_ref, most_ref
):
    group, column = lax.axis_index("dp"), lax.axis_index("tensor") // 2
    count, nodes, model = queries_ref.shape
    kv_heads, width = tree_ref.shape[2], tree_ref.shape[3] // 2
    pick = lax.broadcasted_iota(jnp.int32, (nodes, kv_heads, 2 * width), 1) == column
    for r in range(count):
        packed_ref[r, :, :model] = encode(queries_ref[r].astype(jnp.float32))
        tree = jnp.sum(jnp.where(pick, tree_ref[r].astype(jnp.float32), 0.0), axis=1)
        packed_ref[r, :, model:] = encode(tree)
    requests = holder_ref.shape[1]
    line = lax.broadcasted_iota(jnp.int32, (requests, requests), 0)
    lane = lax.broadcasted_iota(jnp.int32, (requests, requests), 1)
    row = holder_ref[...]
    rows = jnp.broadcast_to(row, (requests, requests))
    column = jnp.sum(jnp.where(line == lane, rows, 0), axis=1, keepdims=True)

    def counted(chosen, axis):
        return jnp.sum(jnp.where(chosen, 1, 0), axis=axis, keepdims=True)

    same, earlier, later = column == rows, line < lane, lane < line
    block = (column >> 3) == (rows >> 3)
    rank, rank_line = counted(same & earlier, 0), counted(same & later, 1)
    place = counted(block & ((column < rows) | (same & earlier)), 0)
    place_line = counted(block & ((rows < column) | (same & later)), 1)
    slot = (place & 7) * 2 + (rank >> 3)
    slot_line = (place_line & 7) * 2 + (rank_line >> 3)
    slot_ref[...] = jnp.where(row == group, slot, -1)
    mine = (column == group) & (slot_line == lane)
    index_ref[...] = jnp.sum(jnp.where(mine, line, 0), axis=0, keepdims=True)
    device = (row >> 3) * BLOCK + (place & 7)
    for k, height in enumerate(ROWS):
        spot_ref[k : k + 1, :] = device * height + (place >> 3)
    kept = ((column >> 3) == (group >> 3)) & (place_line == BLOCK * lane + (group & 7))
    source = (column & 7) * 2 + (rank_line >> 3)
    source_ref[...] = jnp.sum(jnp.where(kept, source, 0), axis=0, keepdims=True)
    most = jnp.max(place, axis=1, keepdims=True) // BLOCK + 1
    choice = sum(jnp.where(most > height, 1, 0) for height in ROWS[:-1])
    most_ref[...] = jnp.broadcast_to(choice, most_ref.shape)


def pack(queries, tree, holder):
    count, nodes, model = queries.shape
    width = tree.shape[3] // 2
    requests = holder.shape[0]
    vmem = pl.BlockSpec(memory_space=pltpu.VMEM)
    line = jax.ShapeDtypeStruct((1, requests), jnp.int32)
    return pl.pallas_call(
        pack_kernel,
        out_shape=(
            jax.ShapeDtypeStruct((count, nodes, model + 2 * width), jnp.float32),
            line,
            line,
            jax.ShapeDtypeStruct((len(ROWS), requests), jnp.int32),
            line,
            line,
        ),
        in_specs=[vmem] * 3,
        out_specs=(vmem,) * 6,
        compiler_params=pltpu.CompilerParams(vmem_limit_bytes=8 * 1024 * 1024),
        name="pack",
    )(queries, tree, holder.reshape(1, requests))


def attend_kernel(slot_ref, parents_ref, picked_ref, own_ref, other_ref, out_ref, reach_ref, value_ref):
    step = pl.program_id(0)
    nodes = picked_ref.shape[1]
    width = own_ref.shape[1] // 2
    heads = (picked_ref.shape[2] - 2 * width) // width
    half = own_ref.shape[0]
    rows = CAP * nodes

    @pl.when(step == 0)
    def _():
        line = lax.broadcasted_iota(jnp.int32, (rows, rows), 0)
        column = lax.broadcasted_iota(jnp.int32, (rows, rows), 1)
        requests = slot_ref.shape[1]
        taken = lax.broadcasted_iota(jnp.int32, (rows, requests), 0) // nodes == slot_ref[...]
        above = lax.dot_general(
            jnp.where(taken, 1.0, 0.0).astype(jnp.bfloat16),
            parents_ref[...].astype(jnp.float32).astype(jnp.bfloat16),
            (((1,), (1,)), ((), ())),
            preferred_element_type=jnp.float32,
        )
        node = lax.broadcasted_iota(jnp.int32, (rows, nodes), 0) % nodes
        own_node = lax.broadcasted_iota(jnp.int32, (rows, nodes), 1) == node
        above = jnp.sum(jnp.where(own_node, above, 0.0), axis=1, keepdims=True).astype(jnp.int32)
        above = (line // nodes) * nodes + above
        reach = jnp.where((column == line) | (column == above), 1.0, 0.0).astype(jnp.bfloat16)
        for level in range(4):
            reach = jnp.minimum(
                jnp.dot(reach, reach, preferred_element_type=jnp.float32), 1.0
            ).astype(jnp.bfloat16)
        reach_ref[...] = reach.astype(jnp.float32)
        value_ref[pl.ds(0, half), :width] = own_ref[:, width:]
        value_ref[pl.ds(half, half), :width] = other_ref[:, width:]
        value_ref[:, width:] = jnp.ones((2 * half, width), jnp.bfloat16)

    scale = 1.0 / math.sqrt(width) * math.log2(math.e)
    query = jnp.concatenate(
        [picked_ref[s, :, h * width : (h + 1) * width] for s in range(PAIR) for h in range(heads)],
        axis=0,
    )
    tree = jnp.concatenate([picked_ref[s, :, heads * width :] for s in range(PAIR)], axis=0)
    dims = (((1,), (1,)), ((), ()))
    span = PAIR * nodes
    mask = jnp.zeros((span, span), jnp.float32)
    for k in range(CAP // PAIR):
        block = reach_ref[k * span : (k + 1) * span, k * span : (k + 1) * span]
        mask = jnp.where(step == k, block, mask)
    mask = jnp.concatenate(
        [mask[s * nodes : (s + 1) * nodes] for s in range(PAIR) for h in range(heads)], axis=0
    )
    drafts = lax.dot_general(query, tree[:, :width], dims, preferred_element_type=jnp.float32)
    drafts = jnp.where(mask > 0, drafts, NEG)
    peak = jnp.max(drafts, axis=1, keepdims=True)
    drafts = (jnp.exp2((drafts - peak) * scale) * mask).astype(jnp.bfloat16)
    tree_value = jnp.concatenate([tree[:, width:], jnp.ones((span, width), jnp.bfloat16)], axis=1)
    peaks = [peak]
    sums = [jnp.dot(drafts, tree_value, preferred_element_type=jnp.float32)]
    for k, ref in enumerate((own_ref, other_ref)):
        scores = lax.dot_general(query, ref[:, :width], dims, preferred_element_type=jnp.float32)
        peak = jnp.max(scores, axis=1, keepdims=True)
        weights = jnp.exp2((scores - peak) * scale).astype(jnp.bfloat16)
        peaks.append(peak)
        sums.append(
            jnp.dot(
                weights, value_ref[pl.ds(k * half, half), :], preferred_element_type=jnp.float32
            )
        )
    top = jnp.maximum(jnp.maximum(peaks[0], peaks[1]), peaks[2])
    summed = sum(jnp.exp2((peak - top) * scale) * part for peak, part in zip(peaks, sums))
    attended = (summed[:, :width] / summed[:, width:]).astype(jnp.bfloat16)
    for s in range(PAIR):
        for h in range(heads):
            start = (s * heads + h) * nodes
            out_ref[s, :, h * width : (h + 1) * width] = attended[start : start + nodes]


def attend(slot, parents, picked, own, other):
    nodes, depth = picked.shape[1:]
    width = own.shape[1] // 2
    half = own.shape[0]
    model = depth - 2 * width
    return pl.pallas_call(
        attend_kernel,
        out_shape=jax.ShapeDtypeStruct((CAP, nodes, model), jnp.bfloat16),
        grid=(CAP // PAIR,),
        in_specs=[
            pl.BlockSpec(slot.shape, lambda i: (0, 0)),
            pl.BlockSpec(parents.shape, lambda i: (0, 0)),
            pl.BlockSpec((PAIR, nodes, depth), lambda i: (i, 0, 0)),
            pl.BlockSpec((half, 2 * width), lambda i: (0, 0)),
            pl.BlockSpec((half, 2 * width), lambda i: (0, 0)),
        ],
        out_specs=pl.BlockSpec((PAIR, nodes, model), lambda i: (i, 0, 0)),
        scratch_shapes=[
            pltpu.VMEM((CAP * nodes, CAP * nodes), jnp.float32),
            pltpu.VMEM((2 * half, 2 * width), jnp.bfloat16),
        ],
        compiler_params=pltpu.CompilerParams(vmem_limit_bytes=24 * 1024 * 1024),
        name="attend",
    )(slot, parents, picked, own, other)


def settle_kernel(source_ref, spread_ref, out_ref):
    for k in range(out_ref.shape[0]):
        out_ref[k] = encode(spread_ref[source_ref[0, k]].astype(jnp.float32))


def settle(source, spread, count):
    vmem = pl.BlockSpec(memory_space=pltpu.VMEM)
    return pl.pallas_call(
        settle_kernel,
        out_shape=jax.ShapeDtypeStruct((count, *spread.shape[1:]), jnp.float32),
        grid_spec=pltpu.PrefetchScalarGridSpec(
            num_scalar_prefetch=1, grid=(), in_specs=[vmem], out_specs=vmem
        ),
        compiler_params=pltpu.CompilerParams(vmem_limit_bytes=12 * 1024 * 1024),
        name="settle",
    )(source, spread)


def project_kernel(choice, spot_ref, every_ref, weight_ref, out_ref):
    lanes = out_ref.shape[0]
    share = spot_ref.shape[1] // lanes
    for lane in range(lanes):
        block = jnp.concatenate(
            [every_ref[spot_ref[choice, lane * share + r]] for r in range(share)], axis=0
        )
        out_ref[lane] = jnp.dot(
            block, weight_ref[...], preferred_element_type=jnp.float32
        ).astype(jnp.bfloat16)


def project(choice, spot, every, weight, lanes):
    requests, nodes = spot.shape[1], every.shape[1]
    columns = weight.shape[1]
    vmem = pl.BlockSpec(memory_space=pltpu.VMEM)
    return pl.pallas_call(
        functools.partial(project_kernel, choice),
        out_shape=jax.ShapeDtypeStruct((lanes, requests // lanes * nodes, columns), jnp.bfloat16),
        grid_spec=pltpu.PrefetchScalarGridSpec(
            num_scalar_prefetch=1, grid=(), in_specs=[vmem] * 2, out_specs=vmem
        ),
        compiler_params=pltpu.CompilerParams(vmem_limit_bytes=16 * 1024 * 1024),
        name="project",
    )(spot, every, weight)


def share_rows(choice, lanes, source, spread, spot, weight):
    settled = settle(source, spread, ROWS[choice])
    every = lax.all_gather(settled.astype(jnp.float16), "dp", axis=0, tiled=True)
    return project(choice, spot, decode(every), weight, lanes)


def local(queries, tree_kv, prefix_kv, request_holder, parents, out_weight):
    lanes = lax.axis_size("tensor")
    groups = lax.axis_size("dp")
    requests = request_holder.shape[0]
    nodes = queries.shape[1]
    own_half = prefix_kv[0, 0]
    other_half = swapped(own_half, "tensor", 0)
    packed, slot, index, spot, source, most = pack(queries, tree_kv, request_holder)
    packed = lax.all_gather(packed.astype(jnp.float16), "dp", axis=0, tiled=True)
    picked = decode(packed.at[index[0, :CAP]].get(mode="promise_in_bounds"))
    attended = attend(slot, parents.T, picked, own_half, other_half)
    blocks = [list(range(i, i + BLOCK)) for i in range(0, groups, BLOCK)]
    spread = lax.all_to_all(attended, "dp", 0, 0, axis_index_groups=blocks, tiled=True)
    partial = lax.switch(
        most[0, 0],
        [functools.partial(share_rows, choice, lanes) for choice in range(len(ROWS))],
        source,
        spread,
        spot,
        out_weight,
    )
    shares = lax.all_to_all(partial, "tensor", 0, 0, tiled=True)
    total = jnp.sum(shares.astype(jnp.float32), axis=0).astype(jnp.bfloat16)
    return total.reshape(requests // lanes, nodes, out_weight.shape[1])


def solution(mesh):
    return jax.shard_map(
        local,
        mesh=mesh,
        in_specs=(
            P("dp", None, "tensor"),
            P("dp", None, None, None),
            P("dp", "tensor", None, None),
            P(),
            P(),
            P("tensor", "dp"),
        ),
        out_specs=P("tensor", None, "dp"),
        check_vma=False,
    )
```

```python
import functools
import math

import jax
import jax.numpy as jnp
from jax import lax
from jax.experimental import pallas as pl
from jax.experimental.pallas import tpu as pltpu
from jax.sharding import PartitionSpec as P

CAP = 16
PAIR = 16
BLOCK = 8
ROWS = (6, 8, 16)
QUAD = 4
NEG = -1e30
LIFT = 2.0**59


def swapped(x, axis, bit):
    return lax.ppermute(x, axis, [(i, i ^ 1 << bit) for i in range(lax.axis_size(axis))])


def turned(x, by):
    lanes = lax.axis_size("tensor")
    pairs = [(i - i % QUAD + (i + by) % QUAD, i) for i in range(lanes)]
    return lax.ppermute(x, "tensor", pairs)


def encode(x):
    root = jnp.sqrt(jnp.sqrt(jnp.abs(x) * LIFT))
    return jnp.where(x < 0, -root, root)


def decode(x):
    x = x.astype(jnp.float32)
    return ((x * jnp.abs(x)) * ((x * (1.0 / LIFT)) * x)).astype(jnp.bfloat16)


def pack_kernel(
    queries_ref, tree_ref, holder_ref, packed_ref, slot_ref, index_ref, spot_ref, source_ref, most_ref
):
    group, column = lax.axis_index("dp"), lax.axis_index("tensor") // 2
    count, nodes, model = queries_ref.shape
    kv_heads, width = tree_ref.shape[2], tree_ref.shape[3] // 2
    pick = lax.broadcasted_iota(jnp.int32, (nodes, kv_heads, 2 * width), 1) == column
    for r in range(count):
        packed_ref[r, :, :model] = encode(queries_ref[r].astype(jnp.float32))
        tree = jnp.sum(jnp.where(pick, tree_ref[r].astype(jnp.float32), 0.0), axis=1)
        packed_ref[r, :, model:] = encode(tree)
    requests = holder_ref.shape[1]
    line = lax.broadcasted_iota(jnp.int32, (requests, requests), 0)
    lane = lax.broadcasted_iota(jnp.int32, (requests, requests), 1)
    row = holder_ref[...]
    rows = jnp.broadcast_to(row, (requests, requests))
    column = jnp.sum(jnp.where(line == lane, rows, 0), axis=1, keepdims=True)

    def counted(chosen, axis):
        return jnp.sum(jnp.where(chosen, 1, 0), axis=axis, keepdims=True)

    same, earlier, later = column == rows, line < lane, lane < line
    block = (column >> 3) == (rows >> 3)
    rank, rank_line = counted(same & earlier, 0), counted(same & later, 1)
    place = counted(block & ((column < rows) | (same & earlier)), 0)
    place_line = counted(block & ((rows < column) | (same & later)), 1)
    slot = (place & 7) * 2 + (rank >> 3)
    slot_line = (place_line & 7) * 2 + (rank_line >> 3)
    slot_ref[...] = jnp.where(row == group, slot, -1)
    mine = (column == group) & (slot_line == lane)
    index_ref[...] = jnp.sum(jnp.where(mine, line, 0), axis=0, keepdims=True)
    device = (row >> 3) * BLOCK + (place & 7)
    for k, height in enumerate(ROWS):
        spot_ref[k : k + 1, :] = device * height + (place >> 3)
    kept = ((column >> 3) == (group >> 3)) & (place_line == BLOCK * lane + (group & 7))
    source = (column & 7) * 2 + (rank_line >> 3)
    source_ref[...] = jnp.sum(jnp.where(kept, source, 0), axis=0, keepdims=True)
    most = jnp.max(place, axis=1, keepdims=True) // BLOCK + 1
    choice = sum(jnp.where(most > height, 1, 0) for height in ROWS[:-1])
    most_ref[...] = jnp.broadcast_to(choice, most_ref.shape)


def pack(queries, tree, holder):
    count, nodes, model = queries.shape
    width = tree.shape[3] // 2
    requests = holder.shape[0]
    vmem = pl.BlockSpec(memory_space=pltpu.VMEM)
    line = jax.ShapeDtypeStruct((1, requests), jnp.int32)
    return pl.pallas_call(
        pack_kernel,
        out_shape=(
            jax.ShapeDtypeStruct((count, nodes, model + 2 * width), jnp.float32),
            line,
            line,
            jax.ShapeDtypeStruct((len(ROWS), requests), jnp.int32),
            line,
            line,
        ),
        in_specs=[vmem] * 3,
        out_specs=(vmem,) * 6,
        compiler_params=pltpu.CompilerParams(vmem_limit_bytes=8 * 1024 * 1024),
        name="pack",
    )(queries, tree, holder.reshape(1, requests))


def attend_kernel(slot_ref, parents_ref, picked_ref, own_ref, other_ref, out_ref, reach_ref, value_ref):
    step = pl.program_id(0)
    nodes = picked_ref.shape[1]
    width = own_ref.shape[1] // 2
    heads = (picked_ref.shape[2] - 2 * width) // width
    half = own_ref.shape[0]
    rows = CAP * nodes

    @pl.when(step == 0)
    def _():
        line = lax.broadcasted_iota(jnp.int32, (rows, rows), 0)
        column = lax.broadcasted_iota(jnp.int32, (rows, rows), 1)
        requests = slot_ref.shape[1]
        taken = lax.broadcasted_iota(jnp.int32, (rows, requests), 0) // nodes == slot_ref[...]
        above = lax.dot_general(
            jnp.where(taken, 1.0, 0.0).astype(jnp.bfloat16),
            parents_ref[...].astype(jnp.float32).astype(jnp.bfloat16),
            (((1,), (1,)), ((), ())),
            preferred_element_type=jnp.float32,
        )
        node = lax.broadcasted_iota(jnp.int32, (rows, nodes), 0) % nodes
        own_node = lax.broadcasted_iota(jnp.int32, (rows, nodes), 1) == node
        above = jnp.sum(jnp.where(own_node, above, 0.0), axis=1, keepdims=True).astype(jnp.int32)
        above = (line // nodes) * nodes + above
        reach = jnp.where((column == line) | (column == above), 1.0, 0.0).astype(jnp.bfloat16)
        for level in range(4):
            reach = jnp.minimum(
                jnp.dot(reach, reach, preferred_element_type=jnp.float32), 1.0
            ).astype(jnp.bfloat16)
        reach_ref[...] = reach.astype(jnp.float32)
        value_ref[pl.ds(0, half), :width] = own_ref[:, width:]
        value_ref[pl.ds(half, half), :width] = other_ref[:, width:]
        value_ref[:, width:] = jnp.ones((2 * half, width), jnp.bfloat16)

    scale = 1.0 / math.sqrt(width) * math.log2(math.e)
    query = jnp.concatenate(
        [picked_ref[s, :, h * width : (h + 1) * width] for s in range(PAIR) for h in range(heads)],
        axis=0,
    )
    tree = jnp.concatenate([picked_ref[s, :, heads * width :] for s in range(PAIR)], axis=0)
    dims = (((1,), (1,)), ((), ()))
    span = PAIR * nodes
    mask = jnp.zeros((span, span), jnp.float32)
    for k in range(CAP // PAIR):
        block = reach_ref[k * span : (k + 1) * span, k * span : (k + 1) * span]
        mask = jnp.where(step == k, block, mask)
    mask = jnp.concatenate(
        [mask[s * nodes : (s + 1) * nodes] for s in range(PAIR) for h in range(heads)], axis=0
    )
    drafts = lax.dot_general(query, tree[:, :width], dims, preferred_element_type=jnp.float32)
    drafts = jnp.where(mask > 0, drafts, NEG)
    peak = jnp.max(drafts, axis=1, keepdims=True)
    drafts = (jnp.exp2((drafts - peak) * scale) * mask).astype(jnp.bfloat16)
    tree_value = jnp.concatenate([tree[:, width:], jnp.ones((span, width), jnp.bfloat16)], axis=1)
    peaks = [peak]
    sums = [jnp.dot(drafts, tree_value, preferred_element_type=jnp.float32)]
    for k, ref in enumerate((own_ref, other_ref)):
        scores = lax.dot_general(query, ref[:, :width], dims, preferred_element_type=jnp.float32)
        peak = jnp.max(scores, axis=1, keepdims=True)
        weights = jnp.exp2((scores - peak) * scale).astype(jnp.bfloat16)
        peaks.append(peak)
        sums.append(
            jnp.dot(
                weights, value_ref[pl.ds(k * half, half), :], preferred_element_type=jnp.float32
            )
        )
    top = jnp.maximum(jnp.maximum(peaks[0], peaks[1]), peaks[2])
    summed = sum(jnp.exp2((peak - top) * scale) * part for peak, part in zip(peaks, sums))
    attended = (summed[:, :width] / summed[:, width:]).astype(jnp.bfloat16)
    for s in range(PAIR):
        for h in range(heads):
            start = (s * heads + h) * nodes
            out_ref[s, :, h * width : (h + 1) * width] = attended[start : start + nodes]


def attend(slot, parents, picked, own, other):
    nodes, depth = picked.shape[1:]
    width = own.shape[1] // 2
    half = own.shape[0]
    model = depth - 2 * width
    return pl.pallas_call(
        attend_kernel,
        out_shape=jax.ShapeDtypeStruct((CAP, nodes, model), jnp.bfloat16),
        grid=(CAP // PAIR,),
        in_specs=[
            pl.BlockSpec(slot.shape, lambda i: (0, 0)),
            pl.BlockSpec(parents.shape, lambda i: (0, 0)),
            pl.BlockSpec((PAIR, nodes, depth), lambda i: (i, 0, 0)),
            pl.BlockSpec((half, 2 * width), lambda i: (0, 0)),
            pl.BlockSpec((half, 2 * width), lambda i: (0, 0)),
        ],
        out_specs=pl.BlockSpec((PAIR, nodes, model), lambda i: (i, 0, 0)),
        scratch_shapes=[
            pltpu.VMEM((CAP * nodes, CAP * nodes), jnp.float32),
            pltpu.VMEM((2 * half, 2 * width), jnp.bfloat16),
        ],
        compiler_params=pltpu.CompilerParams(vmem_limit_bytes=24 * 1024 * 1024),
        name="attend",
    )(slot, parents, picked, own, other)


def interleave(first, second, swap):
    lower = lax.broadcasted_iota(jnp.int32, first.shape, 0) < QUAD
    if swap:
        return jnp.where(lower, pltpu.roll(first, QUAD, 0), second)
    return jnp.where(lower, first, pltpu.roll(second, QUAD, 0))


def settle_kernel(source_ref, spread_ref, out_ref):
    count = out_ref.shape[1] // QUAD
    tiles = [[] for _ in range(QUAD)]
    for k in range(0, count, 2):
        first = spread_ref[source_ref[0, k]].astype(jnp.float32)
        second = spread_ref[source_ref[0, k + 1]].astype(jnp.float32)
        for quarter in range(QUAD):
            at = quarter // 2 * 8
            tiles[quarter].append(
                interleave(first[at : at + 8], second[at : at + 8], quarter % 2 == 1)
            )
    for quarter in range(QUAD):
        out_ref[quarter] = jnp.concatenate(tiles[quarter], axis=0).astype(jnp.bfloat16)


def settle(source, spread, count):
    vmem = pl.BlockSpec(memory_space=pltpu.VMEM)
    return pl.pallas_call(
        settle_kernel,
        out_shape=jax.ShapeDtypeStruct((QUAD, count * QUAD, spread.shape[2]), jnp.bfloat16),
        grid_spec=pltpu.PrefetchScalarGridSpec(
            num_scalar_prefetch=1, grid=(), in_specs=[vmem], out_specs=vmem
        ),
        compiler_params=pltpu.CompilerParams(vmem_limit_bytes=12 * 1024 * 1024),
        name="settle",
    )(source, spread)


def join_kernel(quarters_ref, out_ref):
    depth = quarters_ref.shape[2]
    lane = lax.axis_index("tensor")
    for k in range(QUAD):
        part = quarters_ref[(lane + k) & (QUAD - 1)].astype(jnp.float32)
        out_ref[:, k * depth : (k + 1) * depth] = encode(part)


def join(quarters):
    vmem = pl.BlockSpec(memory_space=pltpu.VMEM)
    rows, depth = quarters.shape[1:]
    return pl.pallas_call(
        join_kernel,
        out_shape=jax.ShapeDtypeStruct((rows, QUAD * depth), jnp.float32),
        in_specs=[vmem],
        out_specs=vmem,
        compiler_params=pltpu.CompilerParams(vmem_limit_bytes=12 * 1024 * 1024),
        name="join",
    )(quarters)


def project_kernel(choice, spot_ref, every_ref, *refs):
    weight_refs, out_ref, sum_ref = refs[:QUAD], refs[QUAD], refs[QUAD + 1]
    depth = weight_refs[0].shape[0]
    requests = spot_ref.shape[1]
    count = requests * QUAD
    line = lax.broadcasted_iota(jnp.int32, (count, requests), 0)
    lane = lax.broadcasted_iota(jnp.int32, (count, requests), 1)
    spots = jnp.broadcast_to(spot_ref[choice : choice + 1, :], (count, requests))
    wanted = jnp.sum(jnp.where((line >> 2) == lane, spots, 0), axis=1, keepdims=True) * QUAD
    wanted = wanted + (lax.broadcasted_iota(jnp.int32, (count, 1), 0) & (QUAD - 1))
    step = 256
    for start in range(0, every_ref.shape[0], step):
        product = sum(
            jnp.dot(
                every_ref[start : start + step, k * depth : (k + 1) * depth],
                ref[...],
                preferred_element_type=jnp.float32,
            )
            for k, ref in enumerate(weight_refs)
        ).astype(jnp.bfloat16)
        column = lax.broadcasted_iota(jnp.int32, (count, step), 1) + start
        chosen = jnp.where(column == wanted, 1.0, 0.0).astype(jnp.bfloat16)
        moved = jnp.dot(chosen, product, preferred_element_type=jnp.float32)
        if start == 0:
            sum_ref[...] = moved
        else:
            sum_ref[...] += moved
    out_ref[...] = sum_ref[...].astype(jnp.bfloat16)


def project(choice, spot, every, weights):
    requests = spot.shape[1]
    columns = weights[0].shape[1]
    vmem = pl.BlockSpec(memory_space=pltpu.VMEM)
    return pl.pallas_call(
        functools.partial(project_kernel, choice),
        out_shape=jax.ShapeDtypeStruct((requests * QUAD, columns), jnp.bfloat16),
        in_specs=[vmem] * (2 + QUAD),
        out_specs=vmem,
        scratch_shapes=[pltpu.VMEM((requests * QUAD, columns), jnp.float32)],
        compiler_params=pltpu.CompilerParams(vmem_limit_bytes=32 * 1024 * 1024),
        name="project",
    )(spot, every, *weights)


def finish_kernel(shares_ref, out_ref):
    requests = out_ref.shape[0]
    lanes = shares_ref.shape[0]
    quarters = [
        sum(shares_ref[lane].astype(jnp.float32) for lane in range(quarter, lanes, QUAD))
        for quarter in range(QUAD)
    ]
    for r in range(requests):
        at = r // 2 * 8
        tiles = [
            interleave(quarters[k][at : at + 8], quarters[k + 1][at : at + 8], r % 2 == 1)
            for k in range(0, QUAD, 2)
        ]
        out_ref[r] = jnp.concatenate(tiles, axis=0).astype(jnp.bfloat16)


def finish(shares, nodes):
    rows, columns = shares.shape[1:]
    vmem = pl.BlockSpec(memory_space=pltpu.VMEM)
    return pl.pallas_call(
        finish_kernel,
        out_shape=jax.ShapeDtypeStruct((rows // QUAD, nodes, columns), jnp.bfloat16),
        in_specs=[vmem],
        out_specs=vmem,
        compiler_params=pltpu.CompilerParams(vmem_limit_bytes=12 * 1024 * 1024),
        name="finish",
    )(shares)


def share_rows(choice, quads, source, spread, spot, *weights):
    quarters = settle(source, spread, ROWS[choice])
    quarters = lax.all_to_all(quarters, "tensor", 0, 0, axis_index_groups=quads, tiled=True)
    joined = join(quarters)
    every = lax.all_gather(joined.astype(jnp.float16), "dp", axis=0, tiled=True)
    return project(choice, spot, decode(every), weights)


def local(queries, tree_kv, prefix_kv, request_holder, parents, out_weight):
    lanes = lax.axis_size("tensor")
    groups = lax.axis_size("dp")
    requests = request_holder.shape[0]
    nodes = queries.shape[1]
    own_half = prefix_kv[0, 0]
    other_half = swapped(own_half, "tensor", 0)
    packed, slot, index, spot, source, most = pack(queries, tree_kv, request_holder)
    packed, out_weight = lax.optimization_barrier((packed, out_weight))
    weights = [out_weight] + [turned(out_weight, by) for by in range(1, QUAD)]
    packed = lax.all_gather(packed.astype(jnp.float16), "dp", axis=0, tiled=True)
    picked = decode(packed.at[index[0, :CAP]].get(mode="promise_in_bounds"))
    attended = attend(slot, parents.T, picked, own_half, other_half)
    blocks = [list(range(i, i + BLOCK)) for i in range(0, groups, BLOCK)]
    spread = lax.all_to_all(attended, "dp", 0, 0, axis_index_groups=blocks, tiled=True)
    quads = [list(range(i, i + QUAD)) for i in range(0, lanes, QUAD)]
    partial = lax.switch(
        most[0, 0],
        [functools.partial(share_rows, choice, quads) for choice in range(len(ROWS))],
        source,
        spread,
        spot,
        *weights,
    )
    partial = partial.reshape(lanes, requests // lanes * QUAD, out_weight.shape[1])
    shares = lax.all_to_all(partial, "tensor", 0, 0, tiled=True)
    return finish(shares, nodes)


def solution(mesh):
    return jax.shard_map(
        local,
        mesh=mesh,
        in_specs=(
            P("dp", None, "tensor"),
            P("dp", None, None, None),
            P("dp", "tensor", None, None),
            P(),
            P(),
            P("tensor", "dp"),
        ),
        out_specs=P("tensor", None, "dp"),
        check_vma=False,
    )
```

```python
import functools
import math

import jax
import jax.numpy as jnp
from jax import lax
from jax.experimental import pallas as pl
from jax.experimental.pallas import tpu as pltpu
from jax.sharding import PartitionSpec as P

CAP = 16
PAIR = 16
BLOCK = 8
ROWS = (6, 7, 8, 16)
HALF = 8
NEG = -1e30
LIFT = 2.0**59


def swapped(x, axis, bit):
    return lax.ppermute(x, axis, [(i, i ^ 1 << bit) for i in range(lax.axis_size(axis))])


def encode(x):
    root = jnp.sqrt(jnp.sqrt(jnp.abs(x) * LIFT))
    return jnp.where(x < 0, -root, root)


def decode(x):
    x = x.astype(jnp.float32)
    return ((x * jnp.abs(x)) * ((x * (1.0 / LIFT)) * x)).astype(jnp.bfloat16)


def pack_kernel(
    queries_ref, tree_ref, holder_ref, packed_ref, slot_ref, index_ref, spot_ref, source_ref, most_ref
):
    group, column = lax.axis_index("dp"), lax.axis_index("tensor") // 2
    count, nodes, model = queries_ref.shape
    kv_heads, width = tree_ref.shape[2], tree_ref.shape[3] // 2
    pick = lax.broadcasted_iota(jnp.int32, (nodes, kv_heads, 2 * width), 1) == column
    for r in range(count):
        packed_ref[r, :, :model] = encode(queries_ref[r].astype(jnp.float32))
        tree = jnp.sum(jnp.where(pick, tree_ref[r].astype(jnp.float32), 0.0), axis=1)
        packed_ref[r, :, model:] = encode(tree)
    requests = holder_ref.shape[1]
    line = lax.broadcasted_iota(jnp.int32, (requests, requests), 0)
    lane = lax.broadcasted_iota(jnp.int32, (requests, requests), 1)
    row = holder_ref[...]
    rows = jnp.broadcast_to(row, (requests, requests))
    column = jnp.sum(jnp.where(line == lane, rows, 0), axis=1, keepdims=True)

    def counted(chosen, axis):
        return jnp.sum(jnp.where(chosen, 1, 0), axis=axis, keepdims=True)

    same, earlier, later = column == rows, line < lane, lane < line
    block = (column >> 3) == (rows >> 3)
    rank, rank_line = counted(same & earlier, 0), counted(same & later, 1)
    place = counted(block & ((column < rows) | (same & earlier)), 0)
    place_line = counted(block & ((rows < column) | (same & later)), 1)
    slot = (place & 7) * 2 + (rank >> 3)
    slot_line = (place_line & 7) * 2 + (rank_line >> 3)
    slot_ref[...] = jnp.where(row == group, slot, -1)
    mine = (column == group) & (slot_line == lane)
    index_ref[...] = jnp.sum(jnp.where(mine, line, 0), axis=0, keepdims=True)
    device = (row >> 3) * BLOCK + (place & 7)
    for k, height in enumerate(ROWS):
        spot_ref[k : k + 1, :] = device * height + (place >> 3)
    kept = ((column >> 3) == (group >> 3)) & (place_line == BLOCK * lane + (group & 7))
    source = (column & 7) * 2 + (rank_line >> 3)
    source_ref[...] = jnp.sum(jnp.where(kept, source, 0), axis=0, keepdims=True)
    most = jnp.max(place, axis=1, keepdims=True) // BLOCK + 1
    choice = sum(jnp.where(most > height, 1, 0) for height in ROWS[:-1])
    most_ref[...] = jnp.broadcast_to(choice, most_ref.shape)


def pack(queries, tree, holder):
    count, nodes, model = queries.shape
    width = tree.shape[3] // 2
    requests = holder.shape[0]
    vmem = pl.BlockSpec(memory_space=pltpu.VMEM)
    line = jax.ShapeDtypeStruct((1, requests), jnp.int32)
    return pl.pallas_call(
        pack_kernel,
        out_shape=(
            jax.ShapeDtypeStruct((count, nodes, model + 2 * width), jnp.float32),
            line,
            line,
            jax.ShapeDtypeStruct((len(ROWS), requests), jnp.int32),
            line,
            line,
        ),
        in_specs=[vmem] * 3,
        out_specs=(vmem,) * 6,
        compiler_params=pltpu.CompilerParams(vmem_limit_bytes=8 * 1024 * 1024),
        name="pack",
    )(queries, tree, holder.reshape(1, requests))


def attend_kernel(slot_ref, parents_ref, picked_ref, own_ref, other_ref, out_ref, reach_ref, value_ref):
    step = pl.program_id(0)
    nodes = picked_ref.shape[1]
    width = own_ref.shape[1] // 2
    heads = (picked_ref.shape[2] - 2 * width) // width
    half = own_ref.shape[0]
    rows = CAP * nodes

    @pl.when(step == 0)
    def _():
        line = lax.broadcasted_iota(jnp.int32, (rows, rows), 0)
        column = lax.broadcasted_iota(jnp.int32, (rows, rows), 1)
        requests = slot_ref.shape[1]
        taken = lax.broadcasted_iota(jnp.int32, (rows, requests), 0) // nodes == slot_ref[...]
        above = lax.dot_general(
            jnp.where(taken, 1.0, 0.0).astype(jnp.bfloat16),
            parents_ref[...].astype(jnp.float32).astype(jnp.bfloat16),
            (((1,), (1,)), ((), ())),
            preferred_element_type=jnp.float32,
        )
        node = lax.broadcasted_iota(jnp.int32, (rows, nodes), 0) % nodes
        own_node = lax.broadcasted_iota(jnp.int32, (rows, nodes), 1) == node
        above = jnp.sum(jnp.where(own_node, above, 0.0), axis=1, keepdims=True).astype(jnp.int32)
        above = (line // nodes) * nodes + above
        reach = jnp.where((column == line) | (column == above), 1.0, 0.0).astype(jnp.bfloat16)
        for level in range(4):
            reach = jnp.minimum(
                jnp.dot(reach, reach, preferred_element_type=jnp.float32), 1.0
            ).astype(jnp.bfloat16)
        reach_ref[...] = reach.astype(jnp.float32)
        value_ref[pl.ds(0, half), :width] = own_ref[:, width:]
        value_ref[pl.ds(half, half), :width] = other_ref[:, width:]
        value_ref[:, width:] = jnp.ones((2 * half, width), jnp.bfloat16)

    scale = 1.0 / math.sqrt(width) * math.log2(math.e)
    query = jnp.concatenate(
        [picked_ref[s, :, h * width : (h + 1) * width] for s in range(PAIR) for h in range(heads)],
        axis=0,
    )
    tree = jnp.concatenate([picked_ref[s, :, heads * width :] for s in range(PAIR)], axis=0)
    dims = (((1,), (1,)), ((), ()))
    span = PAIR * nodes
    mask = jnp.zeros((span, span), jnp.float32)
    for k in range(CAP // PAIR):
        block = reach_ref[k * span : (k + 1) * span, k * span : (k + 1) * span]
        mask = jnp.where(step == k, block, mask)
    mask = jnp.concatenate(
        [mask[s * nodes : (s + 1) * nodes] for s in range(PAIR) for h in range(heads)], axis=0
    )
    drafts = lax.dot_general(query, tree[:, :width], dims, preferred_element_type=jnp.float32)
    drafts = jnp.where(mask > 0, drafts, NEG)
    peak = jnp.max(drafts, axis=1, keepdims=True)
    drafts = (jnp.exp2((drafts - peak) * scale) * mask).astype(jnp.bfloat16)
    tree_value = jnp.concatenate([tree[:, width:], jnp.ones((span, width), jnp.bfloat16)], axis=1)
    peaks = [peak]
    sums = [jnp.dot(drafts, tree_value, preferred_element_type=jnp.float32)]
    for k, ref in enumerate((own_ref, other_ref)):
        scores = lax.dot_general(query, ref[:, :width], dims, preferred_element_type=jnp.float32)
        peak = jnp.max(scores, axis=1, keepdims=True)
        weights = jnp.exp2((scores - peak) * scale).astype(jnp.bfloat16)
        peaks.append(peak)
        sums.append(
            jnp.dot(
                weights, value_ref[pl.ds(k * half, half), :], preferred_element_type=jnp.float32
            )
        )
    top = jnp.maximum(jnp.maximum(peaks[0], peaks[1]), peaks[2])
    summed = sum(jnp.exp2((peak - top) * scale) * part for peak, part in zip(peaks, sums))
    attended = (summed[:, :width] / summed[:, width:]).astype(jnp.bfloat16)
    for s in range(PAIR):
        for h in range(heads):
            start = (s * heads + h) * nodes
            out_ref[s, :, h * width : (h + 1) * width] = attended[start : start + nodes]


def attend(slot, parents, picked, own, other):
    nodes, depth = picked.shape[1:]
    width = own.shape[1] // 2
    half = own.shape[0]
    model = depth - 2 * width
    return pl.pallas_call(
        attend_kernel,
        out_shape=jax.ShapeDtypeStruct((CAP, nodes, model), jnp.bfloat16),
        grid=(CAP // PAIR,),
        in_specs=[
            pl.BlockSpec(slot.shape, lambda i: (0, 0)),
            pl.BlockSpec(parents.shape, lambda i: (0, 0)),
            pl.BlockSpec((PAIR, nodes, depth), lambda i: (i, 0, 0)),
            pl.BlockSpec((half, 2 * width), lambda i: (0, 0)),
            pl.BlockSpec((half, 2 * width), lambda i: (0, 0)),
        ],
        out_specs=pl.BlockSpec((PAIR, nodes, model), lambda i: (i, 0, 0)),
        scratch_shapes=[
            pltpu.VMEM((CAP * nodes, CAP * nodes), jnp.float32),
            pltpu.VMEM((2 * half, 2 * width), jnp.bfloat16),
        ],
        compiler_params=pltpu.CompilerParams(vmem_limit_bytes=24 * 1024 * 1024),
        name="attend",
    )(slot, parents, picked, own, other)


def settle_kernel(source_ref, spread_ref, kept_ref, sent_ref):
    odd = (lax.axis_index("tensor") & 1) == 1
    for k in range(kept_ref.shape[0]):
        rows = spread_ref[source_ref[0, k]].astype(jnp.float32)
        lower, upper = rows[:HALF], rows[HALF:]
        kept_ref[k] = jnp.where(odd, upper, lower).astype(jnp.bfloat16)
        sent_ref[k] = jnp.where(odd, lower, upper).astype(jnp.bfloat16)


def settle(source, spread, count):
    vmem = pl.BlockSpec(memory_space=pltpu.VMEM)
    part = jax.ShapeDtypeStruct((count, HALF, spread.shape[2]), jnp.bfloat16)
    return pl.pallas_call(
        settle_kernel,
        out_shape=(part, part),
        grid_spec=pltpu.PrefetchScalarGridSpec(
            num_scalar_prefetch=1, grid=(), in_specs=[vmem], out_specs=(vmem, vmem)
        ),
        compiler_params=pltpu.CompilerParams(vmem_limit_bytes=12 * 1024 * 1024),
        name="settle",
    )(source, spread)


def join_kernel(kept_ref, got_ref, out_ref):
    depth = kept_ref.shape[2]
    out_ref[:, :, :depth] = encode(kept_ref[...].astype(jnp.float32))
    out_ref[:, :, depth:] = encode(got_ref[...].astype(jnp.float32))


def join(kept, got):
    vmem = pl.BlockSpec(memory_space=pltpu.VMEM)
    count, rows, depth = kept.shape
    return pl.pallas_call(
        join_kernel,
        out_shape=jax.ShapeDtypeStruct((count, rows, 2 * depth), jnp.float32),
        in_specs=[vmem] * 2,
        out_specs=vmem,
        compiler_params=pltpu.CompilerParams(vmem_limit_bytes=12 * 1024 * 1024),
        name="join",
    )(kept, got)


def project_kernel(choice, spot_ref, every_ref, own_ref, other_ref, out_ref):
    depth = own_ref.shape[0]
    requests = spot_ref.shape[1]
    step = 32
    for start in range(0, requests, step):
        block = jnp.concatenate(
            [every_ref[spot_ref[choice, start + r]] for r in range(step)], axis=0
        )
        product = jnp.dot(block[:, :depth], own_ref[...], preferred_element_type=jnp.float32)
        product += jnp.dot(block[:, depth:], other_ref[...], preferred_element_type=jnp.float32)
        out_ref[start * HALF : (start + step) * HALF] = product.astype(jnp.bfloat16)


def project(choice, spot, every, own, other):
    requests = spot.shape[1]
    columns = own.shape[1]
    vmem = pl.BlockSpec(memory_space=pltpu.VMEM)
    return pl.pallas_call(
        functools.partial(project_kernel, choice),
        out_shape=jax.ShapeDtypeStruct((requests * HALF, columns), jnp.bfloat16),
        grid_spec=pltpu.PrefetchScalarGridSpec(
            num_scalar_prefetch=1, grid=(), in_specs=[vmem] * 3, out_specs=vmem
        ),
        compiler_params=pltpu.CompilerParams(vmem_limit_bytes=24 * 1024 * 1024),
        name="project",
    )(spot, every, own, other)


def finish_kernel(shares_ref, out_ref):
    lanes = shares_ref.shape[0]
    for half in range(2):
        total = shares_ref[half].astype(jnp.float32)
        for lane in range(half + 2, lanes, 2):
            total += shares_ref[lane].astype(jnp.float32)
        out_ref[:, half * HALF : (half + 1) * HALF] = total.astype(jnp.bfloat16)


def finish(shares):
    lanes, rows, half, columns = shares.shape
    vmem = pl.BlockSpec(memory_space=pltpu.VMEM)
    return pl.pallas_call(
        finish_kernel,
        out_shape=jax.ShapeDtypeStruct((rows, 2 * half, columns), jnp.bfloat16),
        in_specs=[vmem],
        out_specs=vmem,
        compiler_params=pltpu.CompilerParams(vmem_limit_bytes=12 * 1024 * 1024),
        name="finish",
    )(shares)


def share_rows(choice, source, spread, spot, own, other):
    kept, sent = settle(source, spread, ROWS[choice])
    joined = join(kept, swapped(sent, "tensor", 0))
    every = lax.all_gather(joined.astype(jnp.float16), "dp", axis=0, tiled=True)
    return project(choice, spot, decode(every), own, other)


def local(queries, tree_kv, prefix_kv, request_holder, parents, out_weight):
    lanes = lax.axis_size("tensor")
    groups = lax.axis_size("dp")
    requests = request_holder.shape[0]
    own_half = prefix_kv[0, 0]
    other_half, other_weight = lax.optimization_barrier(
        (swapped(own_half, "tensor", 0), swapped(out_weight, "tensor", 0))
    )
    packed, slot, index, spot, source, most = pack(queries, tree_kv, request_holder)
    packed = lax.all_gather(packed.astype(jnp.float16), "dp", axis=0, tiled=True)
    picked = decode(packed.at[index[0, :CAP]].get(mode="promise_in_bounds"))
    attended = attend(slot, parents.T, picked, own_half, other_half)
    blocks = [list(range(i, i + BLOCK)) for i in range(0, groups, BLOCK)]
    spread = lax.all_to_all(attended, "dp", 0, 0, axis_index_groups=blocks, tiled=True)
    partial = lax.switch(
        most[0, 0],
        [functools.partial(share_rows, choice) for choice in range(len(ROWS))],
        source,
        spread,
        spot,
        out_weight,
        other_weight,
    )
    partial = partial.reshape(lanes, requests // lanes, HALF, out_weight.shape[1])
    return finish(lax.all_to_all(partial, "tensor", 0, 0, tiled=True))


def solution(mesh):
    return jax.shard_map(
        local,
        mesh=mesh,
        in_specs=(
            P("dp", None, "tensor"),
            P("dp", None, None, None),
            P("dp", "tensor", None, None),
            P(),
            P(),
            P("tensor", "dp"),
        ),
        out_specs=P("tensor", None, "dp"),
        check_vma=False,
    )
```

```python
import functools
import math

import jax
import jax.numpy as jnp
from jax import lax
from jax.experimental import pallas as pl
from jax.experimental.pallas import tpu as pltpu
from jax.sharding import PartitionSpec as P

CAP = 16
BLOCK = 8
ROWS = (5, 6, 7, 8, 16)
HALF = 8
NEG = -1e30
LIFT = 2.0**59


def swapped(x, axis, bit):
    return lax.ppermute(x, axis, [(i, i ^ 1 << bit) for i in range(lax.axis_size(axis))])


def encode(x):
    root = jnp.sqrt(jnp.sqrt(jnp.abs(x) * LIFT))
    return jnp.where(x < 0, -root, root)


def decode(x):
    x = x.astype(jnp.float32)
    return ((x * jnp.abs(x)) * ((x * (1.0 / LIFT)) * x)).astype(jnp.bfloat16)


def pack_kernel(
    queries_ref, tree_ref, holder_ref, packed_ref, slot_ref, index_ref, spot_ref, source_ref, most_ref
):
    group, column = lax.axis_index("dp"), lax.axis_index("tensor") // 2
    count, nodes, model = queries_ref.shape
    kv_heads, width = tree_ref.shape[2], tree_ref.shape[3] // 2
    pick = lax.broadcasted_iota(jnp.int32, (nodes, kv_heads, 2 * width), 1) == column
    for r in range(count):
        packed_ref[r, :, :model] = encode(queries_ref[r].astype(jnp.float32))
        tree = jnp.sum(jnp.where(pick, tree_ref[r].astype(jnp.float32), 0.0), axis=1)
        packed_ref[r, :, model:] = encode(tree)
    requests = holder_ref.shape[1]
    line = lax.broadcasted_iota(jnp.int32, (requests, requests), 0)
    lane = lax.broadcasted_iota(jnp.int32, (requests, requests), 1)
    row = holder_ref[...]
    rows = jnp.broadcast_to(row, (requests, requests))
    column = jnp.sum(jnp.where(line == lane, rows, 0), axis=1, keepdims=True)

    def counted(chosen, axis):
        return jnp.sum(jnp.where(chosen, 1, 0), axis=axis, keepdims=True)

    same, earlier, later = column == rows, line < lane, lane < line
    block = (column >> 3) == (rows >> 3)
    rank, rank_line = counted(same & earlier, 0), counted(same & later, 1)
    place = counted(block & ((column < rows) | (same & earlier)), 0)
    place_line = counted(block & ((rows < column) | (same & later)), 1)
    slot = (place & 7) * 2 + (rank >> 3)
    slot_line = (place_line & 7) * 2 + (rank_line >> 3)
    slot_ref[...] = jnp.where(row == group, slot, -1)
    mine = (column == group) & (slot_line == lane)
    index_ref[...] = jnp.sum(jnp.where(mine, line, 0), axis=0, keepdims=True)
    device = (row >> 3) * BLOCK + (place & 7)
    for k, height in enumerate(ROWS):
        spot_ref[k : k + 1, :] = device * height + (place >> 3)
    kept = ((column >> 3) == (group >> 3)) & (place_line == BLOCK * lane + (group & 7))
    source = (column & 7) * 2 + (rank_line >> 3)
    source_ref[...] = jnp.sum(jnp.where(kept, source, 0), axis=0, keepdims=True)
    most = jnp.max(place, axis=1, keepdims=True) // BLOCK + 1
    choice = sum(jnp.where(most > height, 1, 0) for height in ROWS[:-1])
    most_ref[...] = jnp.broadcast_to(choice, most_ref.shape)


def pack(queries, tree, holder):
    count, nodes, model = queries.shape
    width = tree.shape[3] // 2
    requests = holder.shape[0]
    vmem = pl.BlockSpec(memory_space=pltpu.VMEM)
    line = jax.ShapeDtypeStruct((1, requests), jnp.int32)
    return pl.pallas_call(
        pack_kernel,
        out_shape=(
            jax.ShapeDtypeStruct((count, nodes, model + 2 * width), jnp.float32),
            line,
            line,
            jax.ShapeDtypeStruct((len(ROWS), requests), jnp.int32),
            line,
            line,
        ),
        in_specs=[vmem] * 3,
        out_specs=(vmem,) * 6,
        compiler_params=pltpu.CompilerParams(vmem_limit_bytes=8 * 1024 * 1024),
        name="pack",
    )(queries, tree, holder.reshape(1, requests))


def attend_kernel(slot_ref, parents_ref, picked_ref, own_ref, other_ref, out_ref, value_ref):
    nodes = picked_ref.shape[1]
    width = own_ref.shape[1] // 2
    heads = (picked_ref.shape[2] - 2 * width) // width
    half = own_ref.shape[0]
    rows = CAP * nodes
    line = lax.broadcasted_iota(jnp.int32, (rows, rows), 0)
    column = lax.broadcasted_iota(jnp.int32, (rows, rows), 1)
    requests = slot_ref.shape[1]
    taken = lax.broadcasted_iota(jnp.int32, (rows, requests), 0) // nodes == slot_ref[...]
    above = lax.dot_general(
        jnp.where(taken, 1.0, 0.0).astype(jnp.bfloat16),
        parents_ref[...].astype(jnp.float32).astype(jnp.bfloat16),
        (((1,), (1,)), ((), ())),
        preferred_element_type=jnp.float32,
    )
    node = lax.broadcasted_iota(jnp.int32, (rows, nodes), 0) % nodes
    own_node = lax.broadcasted_iota(jnp.int32, (rows, nodes), 1) == node
    above = jnp.sum(jnp.where(own_node, above, 0.0), axis=1, keepdims=True).astype(jnp.int32)
    above = (line // nodes) * nodes + above
    reach = jnp.where((column == line) | (column == above), 1.0, 0.0).astype(jnp.bfloat16)
    for level in range(4):
        reach = jnp.minimum(
            jnp.dot(reach, reach, preferred_element_type=jnp.float32), 1.0
        ).astype(jnp.bfloat16)
    reach = reach.astype(jnp.float32)
    value_ref[pl.ds(0, half), :width] = own_ref[:, width:]
    value_ref[pl.ds(half, half), :width] = other_ref[:, width:]
    value_ref[:, width:] = jnp.ones((2 * half, width), jnp.bfloat16)

    scale = 1.0 / math.sqrt(width) * math.log2(math.e)
    dims = (((1,), (1,)), ((), ()))
    query = jnp.concatenate(
        [picked_ref[s, :, h * width : (h + 1) * width] for s in range(CAP) for h in range(heads)],
        axis=0,
    )
    tops, parts = [], []
    span = BLOCK * nodes
    for start in range(0, CAP, BLOCK):
        slots = range(start, start + BLOCK)
        tree = jnp.concatenate([picked_ref[s, :, heads * width :] for s in slots], axis=0)
        at = start * nodes
        mask = jnp.concatenate(
            [
                reach[s * nodes : (s + 1) * nodes, at : at + span]
                for s in slots
                for h in range(heads)
            ],
            axis=0,
        )
        drafts = lax.dot_general(
            query[at * heads : (at + span) * heads],
            tree[:, :width],
            dims,
            preferred_element_type=jnp.float32,
        )
        drafts = jnp.where(mask > 0, drafts, NEG)
        peak = jnp.max(drafts, axis=1, keepdims=True)
        drafts = (jnp.exp2((drafts - peak) * scale) * mask).astype(jnp.bfloat16)
        value = jnp.concatenate([tree[:, width:], jnp.ones((span, width), jnp.bfloat16)], axis=1)
        tops.append(peak)
        parts.append(jnp.dot(drafts, value, preferred_element_type=jnp.float32))
    peaks = [jnp.concatenate(tops, axis=0)]
    sums = [jnp.concatenate(parts, axis=0)]
    for k, ref in enumerate((own_ref, other_ref)):
        scores = lax.dot_general(query, ref[:, :width], dims, preferred_element_type=jnp.float32)
        peak = jnp.max(scores, axis=1, keepdims=True)
        weights = jnp.exp2((scores - peak) * scale).astype(jnp.bfloat16)
        peaks.append(peak)
        sums.append(
            jnp.dot(
                weights, value_ref[pl.ds(k * half, half), :], preferred_element_type=jnp.float32
            )
        )
    top = jnp.maximum(jnp.maximum(peaks[0], peaks[1]), peaks[2])
    summed = sum(jnp.exp2((peak - top) * scale) * part for peak, part in zip(peaks, sums))
    attended = (summed[:, :width] / summed[:, width:]).astype(jnp.bfloat16)
    for s in range(CAP):
        for h in range(heads):
            start = (s * heads + h) * nodes
            block = attended[start : start + nodes]
            for part in range(2):
                out_ref[s // 2 * 4 + part * 2 + s % 2, :, h * width : (h + 1) * width] = block[
                    part * HALF : (part + 1) * HALF
                ]


def attend(slot, parents, picked, own, other):
    nodes, depth = picked.shape[1:]
    width = own.shape[1] // 2
    model = depth - 2 * width
    vmem = pl.BlockSpec(memory_space=pltpu.VMEM)
    return pl.pallas_call(
        attend_kernel,
        out_shape=jax.ShapeDtypeStruct((CAP * nodes // HALF, HALF, model), jnp.bfloat16),
        in_specs=[vmem] * 5,
        out_specs=vmem,
        scratch_shapes=[pltpu.VMEM((2 * own.shape[0], 2 * width), jnp.bfloat16)],
        compiler_params=pltpu.CompilerParams(vmem_limit_bytes=24 * 1024 * 1024),
        name="attend",
    )(slot, parents, picked, own, other)


def settle_kernel(source_ref, spread_ref, out_ref):
    depth = spread_ref.shape[2]
    lane = lax.axis_index("tensor") & 1
    for k in range(out_ref.shape[0]):
        source = source_ref[0, k]
        for part, side in enumerate((lane, 1 - lane)):
            rows = spread_ref[(source >> 1) * 4 + side * 2 + (source & 1)]
            out_ref[k, :, part * depth : (part + 1) * depth] = encode(rows.astype(jnp.float32))


def settle(source, spread, count):
    vmem = pl.BlockSpec(memory_space=pltpu.VMEM)
    rows, depth = spread.shape[1:]
    return pl.pallas_call(
        settle_kernel,
        out_shape=jax.ShapeDtypeStruct((count, rows, 2 * depth), jnp.float32),
        grid_spec=pltpu.PrefetchScalarGridSpec(
            num_scalar_prefetch=1, grid=(), in_specs=[vmem], out_specs=vmem
        ),
        compiler_params=pltpu.CompilerParams(vmem_limit_bytes=12 * 1024 * 1024),
        name="settle",
    )(source, spread)


def project_kernel(choice, spot_ref, every_ref, own_ref, other_ref, out_ref):
    depth = own_ref.shape[0]
    requests = spot_ref.shape[1]
    step = 32
    for start in range(0, requests, step):
        block = jnp.concatenate(
            [every_ref[spot_ref[choice, start + r]] for r in range(step)], axis=0
        )
        product = jnp.dot(block[:, :depth], own_ref[...], preferred_element_type=jnp.float32)
        product += jnp.dot(block[:, depth:], other_ref[...], preferred_element_type=jnp.float32)
        out_ref[start * HALF : (start + step) * HALF] = product.astype(jnp.bfloat16)


def project(choice, spot, every, own, other):
    requests = spot.shape[1]
    columns = own.shape[1]
    vmem = pl.BlockSpec(memory_space=pltpu.VMEM)
    return pl.pallas_call(
        functools.partial(project_kernel, choice),
        out_shape=jax.ShapeDtypeStruct((requests * HALF, columns), jnp.bfloat16),
        grid_spec=pltpu.PrefetchScalarGridSpec(
            num_scalar_prefetch=1, grid=(), in_specs=[vmem] * 3, out_specs=vmem
        ),
        compiler_params=pltpu.CompilerParams(vmem_limit_bytes=24 * 1024 * 1024),
        name="project",
    )(spot, every, own, other)


def finish_kernel(shares_ref, out_ref):
    lanes = shares_ref.shape[0]
    for half in range(2):
        total = shares_ref[half].astype(jnp.float32)
        for lane in range(half + 2, lanes, 2):
            total += shares_ref[lane].astype(jnp.float32)
        out_ref[:, half * HALF : (half + 1) * HALF] = total.astype(jnp.bfloat16)


def finish(shares):
    lanes, rows, half, columns = shares.shape
    vmem = pl.BlockSpec(memory_space=pltpu.VMEM)
    return pl.pallas_call(
        finish_kernel,
        out_shape=jax.ShapeDtypeStruct((rows, 2 * half, columns), jnp.bfloat16),
        in_specs=[vmem],
        out_specs=vmem,
        compiler_params=pltpu.CompilerParams(vmem_limit_bytes=12 * 1024 * 1024),
        name="finish",
    )(shares)


def share_rows(choice, source, spread, spot, own, other):
    settled = settle(source, spread, ROWS[choice])
    every = lax.all_gather(settled.astype(jnp.float16), "dp", axis=0, tiled=True)
    return project(choice, spot, decode(every), own, other)


def local(queries, tree_kv, prefix_kv, request_holder, parents, out_weight):
    lanes = lax.axis_size("tensor")
    groups = lax.axis_size("dp")
    requests = request_holder.shape[0]
    own_half = prefix_kv[0, 0]
    other_half, other_weight = lax.optimization_barrier(
        (swapped(own_half, "tensor", 0), swapped(out_weight, "tensor", 0))
    )
    packed, slot, index, spot, source, most = pack(queries, tree_kv, request_holder)
    packed = lax.all_gather(packed.astype(jnp.float16), "dp", axis=0, tiled=True)
    picked = decode(packed.at[index[0, :CAP]].get(mode="promise_in_bounds"))
    attended = attend(slot, parents.T, picked, own_half, other_half)
    teams = [
        [(start + k) * lanes + pair + side for k in range(BLOCK) for side in range(2)]
        for start in range(0, groups, BLOCK)
        for pair in range(0, lanes, 2)
    ]
    spread = lax.all_to_all(
        attended, ("dp", "tensor"), 0, 0, axis_index_groups=teams, tiled=True
    )
    partial = lax.switch(
        most[0, 0],
        [functools.partial(share_rows, choice) for choice in range(len(ROWS))],
        source,
        spread,
        spot,
        out_weight,
        other_weight,
    )
    partial = partial.reshape(lanes, requests // lanes, HALF, out_weight.shape[1])
    return finish(lax.all_to_all(partial, "tensor", 0, 0, tiled=True))


def solution(mesh):
    return jax.shard_map(
        local,
        mesh=mesh,
        in_specs=(
            P("dp", None, "tensor"),
            P("dp", None, None, None),
            P("dp", "tensor", None, None),
            P(),
            P(),
            P("tensor", "dp"),
        ),
        out_specs=P("tensor", None, "dp"),
        check_vma=False,
    )
```

```python
import functools
import math

import jax
import jax.numpy as jnp
from jax import lax
from jax.experimental import pallas as pl
from jax.experimental.pallas import tpu as pltpu
from jax.sharding import PartitionSpec as P

CAP = 16
BLOCK = 8
ROWS = (6, 8, 16)
HALF = 8
NEG = -1e30
LIFT = 2.0**59


def swapped(x, axis, bit):
    return lax.ppermute(x, axis, [(i, i ^ 1 << bit) for i in range(lax.axis_size(axis))])


def encode(x):
    root = jnp.sqrt(jnp.sqrt(jnp.abs(x) * LIFT))
    return jnp.where(x < 0, -root, root)


def decode(x):
    x = x.astype(jnp.float32)
    return ((x * jnp.abs(x)) * ((x * (1.0 / LIFT)) * x)).astype(jnp.bfloat16)


def pack_kernel(
    queries_ref, tree_ref, holder_ref, packed_ref, slot_ref, index_ref, spot_ref, source_ref, most_ref
):
    group, column = lax.axis_index("dp"), lax.axis_index("tensor") // 2
    count, nodes, model = queries_ref.shape
    kv_heads, width = tree_ref.shape[2], tree_ref.shape[3] // 2
    pick = lax.broadcasted_iota(jnp.int32, (nodes, kv_heads, 2 * width), 1) == column
    for r in range(count):
        packed_ref[r, :, :model] = encode(queries_ref[r].astype(jnp.float32))
        tree = jnp.sum(jnp.where(pick, tree_ref[r].astype(jnp.float32), 0.0), axis=1)
        packed_ref[r, :, model:] = encode(tree)
    requests = holder_ref.shape[1]
    line = lax.broadcasted_iota(jnp.int32, (requests, requests), 0)
    lane = lax.broadcasted_iota(jnp.int32, (requests, requests), 1)
    row = holder_ref[...]
    rows = jnp.broadcast_to(row, (requests, requests))
    column = jnp.sum(jnp.where(line == lane, rows, 0), axis=1, keepdims=True)

    def counted(chosen, axis):
        return jnp.sum(jnp.where(chosen, 1, 0), axis=axis, keepdims=True)

    same, earlier, later = column == rows, line < lane, lane < line
    block = (column >> 3) == (rows >> 3)
    rank, rank_line = counted(same & earlier, 0), counted(same & later, 1)
    place = counted(block & ((column < rows) | (same & earlier)), 0)
    place_line = counted(block & ((rows < column) | (same & later)), 1)
    slot = (place & 7) * 2 + (rank >> 3)
    slot_line = (place_line & 7) * 2 + (rank_line >> 3)
    slot_ref[...] = jnp.where(row == group, slot, -1)
    mine = (column == group) & (slot_line == lane)
    index_ref[...] = jnp.sum(jnp.where(mine, line, 0), axis=0, keepdims=True)
    device = (row >> 3) * BLOCK + (place & 7)
    for k, height in enumerate(ROWS):
        spot_ref[k : k + 1, :] = device * height + (place >> 3)
    kept = ((column >> 3) == (group >> 3)) & (place_line == BLOCK * lane + (group & 7))
    source = (column & 7) * 2 + (rank_line >> 3)
    source_ref[...] = jnp.sum(jnp.where(kept, source, 0), axis=0, keepdims=True)
    most = jnp.max(place, axis=1, keepdims=True) // BLOCK + 1
    choice = sum(jnp.where(most > height, 1, 0) for height in ROWS[:-1])
    most_ref[...] = jnp.broadcast_to(choice, most_ref.shape)


def pack(queries, tree, holder):
    count, nodes, model = queries.shape
    width = tree.shape[3] // 2
    requests = holder.shape[0]
    vmem = pl.BlockSpec(memory_space=pltpu.VMEM)
    line = jax.ShapeDtypeStruct((1, requests), jnp.int32)
    return pl.pallas_call(
        pack_kernel,
        out_shape=(
            jax.ShapeDtypeStruct((count, nodes, model + 2 * width), jnp.float32),
            line,
            line,
            jax.ShapeDtypeStruct((len(ROWS), requests), jnp.int32),
            line,
            line,
        ),
        in_specs=[vmem] * 3,
        out_specs=(vmem,) * 6,
        compiler_params=pltpu.CompilerParams(vmem_limit_bytes=8 * 1024 * 1024),
        name="pack",
    )(queries, tree, holder.reshape(1, requests))


def attend_kernel(slot_ref, parents_ref, picked_ref, own_ref, other_ref, out_ref, value_ref):
    nodes = picked_ref.shape[1]
    width = own_ref.shape[1] // 2
    heads = (picked_ref.shape[2] - 2 * width) // width
    half = own_ref.shape[0]
    rows = CAP * nodes
    line = lax.broadcasted_iota(jnp.int32, (rows, rows), 0)
    column = lax.broadcasted_iota(jnp.int32, (rows, rows), 1)
    requests = slot_ref.shape[1]
    taken = lax.broadcasted_iota(jnp.int32, (rows, requests), 0) // nodes == slot_ref[...]
    above = lax.dot_general(
        jnp.where(taken, 1.0, 0.0).astype(jnp.bfloat16),
        parents_ref[...].astype(jnp.float32).astype(jnp.bfloat16),
        (((1,), (1,)), ((), ())),
        preferred_element_type=jnp.float32,
    )
    node = lax.broadcasted_iota(jnp.int32, (rows, nodes), 0) % nodes
    own_node = lax.broadcasted_iota(jnp.int32, (rows, nodes), 1) == node
    above = jnp.sum(jnp.where(own_node, above, 0.0), axis=1, keepdims=True).astype(jnp.int32)
    above = (line // nodes) * nodes + above
    reach = jnp.where((column == line) | (column == above), 1.0, 0.0).astype(jnp.bfloat16)
    for level in range(4):
        reach = jnp.minimum(
            jnp.dot(reach, reach, preferred_element_type=jnp.float32), 1.0
        ).astype(jnp.bfloat16)
    reach = reach.astype(jnp.float32)
    value_ref[pl.ds(0, half), :width] = own_ref[:, width:]
    value_ref[pl.ds(half, half), :width] = other_ref[:, width:]
    value_ref[:, width:] = jnp.ones((2 * half, width), jnp.bfloat16)

    scale = 1.0 / math.sqrt(width) * math.log2(math.e)
    dims = (((1,), (1,)), ((), ()))
    query = jnp.concatenate(
        [picked_ref[s, :, h * width : (h + 1) * width] for s in range(CAP) for h in range(heads)],
        axis=0,
    )
    tops, parts = [], []
    span = BLOCK * nodes
    for start in range(0, CAP, BLOCK):
        slots = range(start, start + BLOCK)
        tree = jnp.concatenate([picked_ref[s, :, heads * width :] for s in slots], axis=0)
        at = start * nodes
        mask = jnp.concatenate(
            [
                reach[s * nodes : (s + 1) * nodes, at : at + span]
                for s in slots
                for h in range(heads)
            ],
            axis=0,
        )
        drafts = lax.dot_general(
            query[at * heads : (at + span) * heads],
            tree[:, :width],
            dims,
            preferred_element_type=jnp.float32,
        )
        drafts = jnp.where(mask > 0, drafts, NEG)
        peak = jnp.max(drafts, axis=1, keepdims=True)
        drafts = (jnp.exp2((drafts - peak) * scale) * mask).astype(jnp.bfloat16)
        value = jnp.concatenate([tree[:, width:], jnp.ones((span, width), jnp.bfloat16)], axis=1)
        tops.append(peak)
        parts.append(jnp.dot(drafts, value, preferred_element_type=jnp.float32))
    peaks = [jnp.concatenate(tops, axis=0)]
    sums = [jnp.concatenate(parts, axis=0)]
    for k, ref in enumerate((own_ref, other_ref)):
        scores = lax.dot_general(query, ref[:, :width], dims, preferred_element_type=jnp.float32)
        peak = jnp.max(scores, axis=1, keepdims=True)
        weights = jnp.exp2((scores - peak) * scale).astype(jnp.bfloat16)
        peaks.append(peak)
        sums.append(
            jnp.dot(
                weights, value_ref[pl.ds(k * half, half), :], preferred_element_type=jnp.float32
            )
        )
    top = jnp.maximum(jnp.maximum(peaks[0], peaks[1]), peaks[2])
    summed = sum(jnp.exp2((peak - top) * scale) * part for peak, part in zip(peaks, sums))
    attended = (summed[:, :width] / summed[:, width:]).astype(jnp.bfloat16)
    for s in range(CAP):
        for h in range(heads):
            start = (s * heads + h) * nodes
            block = attended[start : start + nodes]
            for part in range(2):
                out_ref[s // 2 * 4 + part * 2 + s % 2, :, h * width : (h + 1) * width] = block[
                    part * HALF : (part + 1) * HALF
                ]


def attend(slot, parents, picked, own, other):
    nodes, depth = picked.shape[1:]
    width = own.shape[1] // 2
    model = depth - 2 * width
    vmem = pl.BlockSpec(memory_space=pltpu.VMEM)
    return pl.pallas_call(
        attend_kernel,
        out_shape=jax.ShapeDtypeStruct((CAP * nodes // HALF, HALF, model), jnp.bfloat16),
        in_specs=[vmem] * 5,
        out_specs=vmem,
        scratch_shapes=[pltpu.VMEM((2 * own.shape[0], 2 * width), jnp.bfloat16)],
        compiler_params=pltpu.CompilerParams(vmem_limit_bytes=24 * 1024 * 1024),
        name="attend",
    )(slot, parents, picked, own, other)


def settle_kernel(source_ref, spread_ref, out_ref):
    depth = spread_ref.shape[2]
    lane = lax.axis_index("tensor") & 1
    for k in range(out_ref.shape[0]):
        source = source_ref[0, k]
        for part, side in enumerate((lane, 1 - lane)):
            rows = spread_ref[(source >> 1) * 4 + side * 2 + (source & 1)]
            out_ref[k, :, part * depth : (part + 1) * depth] = encode(rows.astype(jnp.float32))


def settle(source, spread, count):
    vmem = pl.BlockSpec(memory_space=pltpu.VMEM)
    rows, depth = spread.shape[1:]
    return pl.pallas_call(
        settle_kernel,
        out_shape=jax.ShapeDtypeStruct((count, rows, 2 * depth), jnp.float32),
        grid_spec=pltpu.PrefetchScalarGridSpec(
            num_scalar_prefetch=1, grid=(), in_specs=[vmem], out_specs=vmem
        ),
        compiler_params=pltpu.CompilerParams(vmem_limit_bytes=12 * 1024 * 1024),
        name="settle",
    )(source, spread)


def project_kernel(choice, spot_ref, every_ref, own_ref, other_ref, out_ref):
    depth = own_ref.shape[0]
    requests = spot_ref.shape[1]
    step = 32

    @pl.loop(0, requests // step)
    def _(turn):
        start = turn * step
        block = jnp.concatenate(
            [every_ref[spot_ref[choice, start + r]] for r in range(step)], axis=0
        )
        product = jnp.dot(block[:, :depth], own_ref[...], preferred_element_type=jnp.float32)
        product += jnp.dot(block[:, depth:], other_ref[...], preferred_element_type=jnp.float32)
        at = pl.multiple_of(start * HALF, step * HALF)
        out_ref[pl.ds(at, step * HALF)] = product.astype(jnp.bfloat16)


def project(choice, spot, every, own, other):
    requests = spot.shape[1]
    columns = own.shape[1]
    vmem = pl.BlockSpec(memory_space=pltpu.VMEM)
    return pl.pallas_call(
        functools.partial(project_kernel, choice),
        out_shape=jax.ShapeDtypeStruct((requests * HALF, columns), jnp.bfloat16),
        grid_spec=pltpu.PrefetchScalarGridSpec(
            num_scalar_prefetch=1, grid=(), in_specs=[vmem] * 3, out_specs=vmem
        ),
        compiler_params=pltpu.CompilerParams(vmem_limit_bytes=24 * 1024 * 1024),
        name="project",
    )(spot, every, own, other)


def finish_kernel(shares_ref, out_ref):
    lanes = shares_ref.shape[0]
    for half in range(2):
        total = shares_ref[half].astype(jnp.float32)
        for lane in range(half + 2, lanes, 2):
            total += shares_ref[lane].astype(jnp.float32)
        out_ref[:, half * HALF : (half + 1) * HALF] = total.astype(jnp.bfloat16)


def finish(shares):
    lanes, rows, half, columns = shares.shape
    vmem = pl.BlockSpec(memory_space=pltpu.VMEM)
    return pl.pallas_call(
        finish_kernel,
        out_shape=jax.ShapeDtypeStruct((rows, 2 * half, columns), jnp.bfloat16),
        in_specs=[vmem],
        out_specs=vmem,
        compiler_params=pltpu.CompilerParams(vmem_limit_bytes=12 * 1024 * 1024),
        name="finish",
    )(shares)


def share_rows(choice, source, spread, spot, own, other):
    settled = settle(source, spread, ROWS[choice])
    every = lax.all_gather(settled.astype(jnp.float16), "dp", axis=0, tiled=True)
    return project(choice, spot, decode(every), own, other)


def local(queries, tree_kv, prefix_kv, request_holder, parents, out_weight):
    lanes = lax.axis_size("tensor")
    groups = lax.axis_size("dp")
    requests = request_holder.shape[0]
    own_half = prefix_kv[0, 0]
    other_half, other_weight = lax.optimization_barrier(
        (swapped(own_half, "tensor", 0), swapped(out_weight, "tensor", 0))
    )
    packed, slot, index, spot, source, most = pack(queries, tree_kv, request_holder)
    packed = lax.all_gather(packed.astype(jnp.float16), "dp", axis=0, tiled=True)
    picked = decode(packed.at[index[0, :CAP]].get(mode="promise_in_bounds"))
    attended = attend(slot, parents.T, picked, own_half, other_half)
    teams = [
        [(start + k) * lanes + pair + side for k in range(BLOCK) for side in range(2)]
        for start in range(0, groups, BLOCK)
        for pair in range(0, lanes, 2)
    ]
    spread = lax.all_to_all(
        attended, ("dp", "tensor"), 0, 0, axis_index_groups=teams, tiled=True
    )
    partial = lax.switch(
        most[0, 0],
        [functools.partial(share_rows, choice) for choice in range(len(ROWS))],
        source,
        spread,
        spot,
        out_weight,
        other_weight,
    )
    partial = partial.reshape(lanes, requests // lanes, HALF, out_weight.shape[1])
    return finish(lax.all_to_all(partial, "tensor", 0, 0, tiled=True))


def solution(mesh):
    return jax.shard_map(
        local,
        mesh=mesh,
        in_specs=(
            P("dp", None, "tensor"),
            P("dp", None, None, None),
            P("dp", "tensor", None, None),
            P(),
            P(),
            P("tensor", "dp"),
        ),
        out_specs=P("tensor", None, "dp"),
        check_vma=False,
    )
```
